128 devices in a mesh: section: 4 (over z), dp: 4 (over x), seq: 8 (over y, core).
Axes of the slice: x: 4, y: 4, z: 4, core: 2. Of those that a mesh axis runs over, the one named last changes fastest.
Arguments:
- block_input: bfloat16 [8, 1024, 1280], P('dp', 'seq', 'section'), may hold values from -6 to 6
- cotangent: bfloat16 [8, 1024, 1280], P('dp', 'seq', 'section'), may hold values from -6 to 6
- cell_lengths: int32 [8, 5], replicated, may hold values from 1 to 1020, as said below
- norm_attn_gain: bfloat16 [4, 1280], P('section', ('dp', 'seq')), may hold values from 0.5 to 1.5
- norm_attn_bias: bfloat16 [4, 1280], P('section', ('dp', 'seq')), may hold values from -1 to 1
- w_qkv: bfloat16 [4, 1280, 3840], P('section', ('dp', 'seq')), may hold values from -0.15625 to 0.15625
- w_out: bfloat16 [4, 1280, 1280], P('section', ('dp', 'seq')), may hold values from -1.25 to 1.25
- norm_ffn_gain: bfloat16 [4, 1280], P('section', ('dp', 'seq')), may hold values from 0.5 to 1.5
- norm_ffn_bias: bfloat16 [4, 1280], P('section', ('dp', 'seq')), may hold values from -1 to 1
- w_up: bfloat16 [4, 1280, 5120], P('section', ('dp', 'seq')), may hold values from -0.15625 to 0.15625
- w_down: bfloat16 [4, 5120, 1280], P('section', ('dp', 'seq')), may hold values from -0.078125 to 0.078125
Outputs:
- block_output: bfloat16 [8, 1024, 1280], P('dp', 'seq', 'section')
- input_grad: float32 [8, 1024, 1280], P('dp', 'seq', 'section')
- grad_norm_attn_gain: float32 [4, 1280], P('section', ('dp', 'seq'))
- grad_norm_attn_bias: float32 [4, 1280], P('section', ('dp', 'seq'))
- grad_w_qkv: float32 [4, 1280, 3840], P('section', ('dp', 'seq'))
- grad_w_out: float32 [4, 1280, 1280], P('section', ('dp', 'seq'))
- grad_norm_ffn_gain: float32 [4, 1280], P('section', ('dp', 'seq'))
- grad_norm_ffn_bias: float32 [4, 1280], P('section', ('dp', 'seq'))
- grad_w_up: float32 [4, 1280, 5120], P('section', ('dp', 'seq'))
- grad_w_down: float32 [4, 5120, 1280], P('section', ('dp', 'seq'))
The draws below stay inside these ranges and needn't reach their ends.
Inputs may be any that keep to these rules, and one draw needn't show every extreme that they name: `cell_lengths`: each micro-batch's 5 cell lengths, in packed order, sum to 1024. Among the 2 micro-batches of each index of dp, one holds a cell of 1020 rows.
All inputs are finite; a program needn't handle non-finite values.
Results may differ from the reference program's by a relative error of at most 0.025.
Values may be sent and summed in bfloat16 or wider, within the bound.
No kernel may reach another device: no remote copies, remote signals or barrier semaphores. Data moves between devices by JAX's collectives and lax.ppermute only.
A program may use at most 448 MiB of HBM per device.

```python
import jax
import jax.numpy as jnp
from jax import lax

D = 1280
HEADS = 20
HEAD_DIM = 64
FF = 5120
LAYERS = 4
ROWS = 1024
CELLS = 5
MICRO = 2
MBS = 8


def draw_cell_lengths(key, part):
    key = jax.random.fold_in(key, 7)
    cut_key, pick_key, lead_key = jax.random.split(key, 3)
    cut_keys = jax.random.split(cut_key, MBS)

    def random_cuts(one_key):
        order = jax.random.permutation(one_key, ROWS - 1) + 1
        cuts = jnp.sort(order[:CELLS - 1]).astype(jnp.int32)
        bounds = jnp.concatenate([jnp.zeros((1,), jnp.int32), cuts, jnp.full((1,), ROWS, jnp.int32)])
        return bounds[1:] - bounds[:-1]
    scattered = jax.vmap(random_cuts)(cut_keys)
    groups = MBS // MICRO
    chosen = jax.random.randint(pick_key, (groups,), 0, MICRO)
    leading = jax.random.randint(lead_key, (groups,), 0, CELLS)
    slots = jnp.arange(CELLS, dtype=jnp.int32)
    spanning = jnp.where(slots[None, :] == leading[:, None], ROWS - CELLS + 1, 1).astype(jnp.int32)
    micro_ids = jnp.arange(MBS, dtype=jnp.int32)
    owners = micro_ids // MICRO
    is_chosen = micro_ids % MICRO == chosen[owners]
    lengths = jnp.where(is_chosen[:, None], spanning[owners], scattered)
    return lengths.astype(jnp.int32)


def levels(key, dims, pieces, least, largest):
    level, own = 1.0, jax.random.fold_in(key, 6)
    for axis_at, shards_of in pieces:
        steps = jnp.exp(jax.random.uniform(jax.random.fold_in(own, axis_at), (shards_of,), jnp.float32, least / len(pieces), largest / len(pieces)))
        level = level * jnp.repeat(steps, dims[axis_at] // shards_of).reshape([-1 if axis == axis_at else 1 for axis in range(len(dims))])
    return level


def gaussian(stream_key, dims, scale, limit, cuts=(), kind=jnp.bfloat16):
    values = jax.random.normal(stream_key, dims, jnp.float32) * scale
    if len(cuts) > 0:
        values = levels(stream_key, dims, cuts, -0.22, 0.18) * values
    return jnp.clip(values, min=-limit, max=limit).astype(kind)


def setup_inputs(seed: int = 0) -> dict:
    streams_of = jax.random.split(jax.random.key(seed), 12)
    return {
        "block_input": gaussian(streams_of[0], (MBS, ROWS, D), 1.0, 6.0, ((0, 4), (1, 8), (2, 4))),
        "cotangent": gaussian(streams_of[1], (MBS, ROWS, D), 1.0, 6.0, ((0, 4), (1, 8), (2, 4))),
        "cell_lengths": draw_cell_lengths(jax.random.fold_in(streams_of[11], 71), 0),
        "norm_attn_gain": jnp.clip(1.0 + 0.1 * jax.random.normal(streams_of[3], (LAYERS, D), jnp.float32), 0.5, 1.5).astype(jnp.bfloat16),
        "norm_attn_bias": gaussian(streams_of[4], (LAYERS, D), 0.2, 1.0, ((0, 4), (1, 32))),
        "w_qkv": gaussian(streams_of[5], (LAYERS, D, 3 * D), D ** -0.5, 0.15625, ((0, 4), (1, 32))),
        "w_out": gaussian(streams_of[6], (LAYERS, D, D), (D // 64) ** -0.5, 1.25, ((0, 4), (1, 32))),
        "norm_ffn_gain": jnp.clip(1.0 + 0.1 * jax.random.normal(streams_of[7], (LAYERS, D), jnp.float32), 0.5, 1.5).astype(jnp.bfloat16),
        "norm_ffn_bias": gaussian(streams_of[8], (LAYERS, D), 0.2, 1.0, ((0, 4), (1, 32))),
        "w_up": gaussian(streams_of[9], (LAYERS, D, FF), D ** -0.5, 0.15625, ((0, 4), (1, 32))),
        "w_down": gaussian(streams_of[10], (LAYERS, FF, D), FF ** -0.5, 0.078125, ((0, 4), (1, 32))),
    }


@jax.custom_vjp
def low(v):
    return lax.optimization_barrier(v.astype(jnp.bfloat16)).astype(jnp.float32)

@jax.custom_vjp
def low_back(v):
    return v

def low_keep(v):
    return (low(v), None)

def low_pass(kept, grad):
    return (grad,)

def back_keep(v):
    return (v, None)

def back_low(kept, grad):
    return (low(grad),)
low.defvjp(low_keep, low_pass)
low_back.defvjp(back_keep, back_low)
EPSILON = 1e-05
MASKED = -1e+30
PRECISE = lax.Precision.HIGHEST

def product(left, right):
    return jnp.dot(left, right, preferred_element_type=jnp.float32, precision=PRECISE)

def layer_norm(values, gain_row, bias_row):
    centered = values - lax.optimization_barrier(jnp.mean(values, axis=-1, keepdims=True))
    spread = lax.optimization_barrier(jnp.mean(centered * centered, axis=-1, keepdims=True))
    return centered * lax.rsqrt(spread + EPSILON) * gain_row + bias_row

def segment_ids(lengths):
    bounds = jnp.cumsum(lengths).astype(jnp.int32)
    places = jnp.arange(ROWS, dtype=jnp.int32)
    return lax.optimization_barrier(jnp.sum((places[:, None] >= bounds[None, :]).astype(jnp.int32), axis=1))

def attend(queries, keys_all, values_all, segments):
    block_rows = min(512, ROWS)
    scaling = HEAD_DIM ** (-0.5)
    key_heads = keys_all.reshape(ROWS, HEADS, HEAD_DIM)
    value_heads = values_all.reshape(ROWS, HEADS, HEAD_DIM)
    query_blocks = queries.reshape(ROWS // block_rows, block_rows, HEADS, HEAD_DIM)
    segment_blocks = segments.reshape(ROWS // block_rows, block_rows)

    def one_block(operands):
        query_part, segment_part = operands
        scores = jnp.einsum('qhd,khd->hqk', query_part, key_heads, precision=PRECISE) * scaling
        allowed = segment_part[:, None] == segments[None, :]
        scores = low_back(jnp.where(allowed[None], scores, MASKED))
        soft_probs = low(jax.nn.softmax(scores, axis=-1))
        return jnp.einsum('hqk,khd->qhd', soft_probs, value_heads, precision=PRECISE)
    attended = lax.map(jax.checkpoint(one_block), (query_blocks, segment_blocks))
    return attended.reshape(ROWS, HEADS * HEAD_DIM)

def block_layer(hidden, params, segments):
    gain_attn, bias_attn, mat_qkv, mat_out, gain_ffn, bias_ffn, mat_up, mat_down = params
    normed = low(layer_norm(hidden, gain_attn, bias_attn))
    projected = low(low_back(product(normed, mat_qkv)))
    attended = low(low_back(attend(projected[:, :D], projected[:, D:2 * D], projected[:, 2 * D:], segments)))
    middle = hidden + low_back(product(attended, mat_out))
    normed_ffn = low(layer_norm(middle, gain_ffn, bias_ffn))
    upward = low_back(product(normed_ffn, mat_up))
    activated = low(jax.nn.gelu(upward, approximate=False))
    result = middle + low_back(product(activated, mat_down))
    return low(low_back(result))

def reference(block_input, cotangent, cell_lengths, norm_attn_gain, norm_attn_bias, w_qkv, w_out, norm_ffn_gain, norm_ffn_bias, w_up, w_down):
    weights = tuple((member.astype(jnp.float32) for member in (norm_attn_gain, norm_attn_bias, w_qkv, w_out, norm_ffn_gain, norm_ffn_bias, w_up, w_down)))

    def forward(hidden, params, segments):
        for layer_index in range(LAYERS):
            hidden = block_layer(hidden, tuple((member[layer_index] for member in params)), segments)
        return hidden

    def micro_step(totals, operands):
        inputs_one, cot_one, lengths = operands
        segments = segment_ids(lengths)
        result, pullback = jax.vjp(lambda hidden, params: forward(hidden, params, segments), inputs_one.astype(jnp.float32), weights)
        grad_hidden, grad_params = pullback(cot_one.astype(jnp.float32))
        totals = tuple((running + addend for running, addend in zip(totals, grad_params)))
        return (totals, (result.astype(jnp.bfloat16), grad_hidden))
    starts = tuple((jnp.zeros(member.shape, jnp.float32) for member in weights))
    totals, (outputs_all, input_grads) = lax.scan(micro_step, starts, (block_input, cotangent, cell_lengths))
    return (outputs_all, input_grads, totals[0], totals[1], totals[2], totals[3], totals[4], totals[5], totals[6], totals[7])
```

```python
import functools
import math

import jax
import jax.numpy as jnp
from jax import lax
from jax.experimental import pallas as pl
from jax.experimental.pallas import tpu as pltpu
from jax.sharding import Mesh, PartitionSpec as P

HEAD_DIM = 64
EPSILON = 1e-05
MASKED = -1e30
BF = jnp.bfloat16
F32 = jnp.float32
VMEM_LIMIT = 20 * 1024 * 1024


def moved(value, axis, steps):
    count = lax.axis_size(axis)
    return lax.ppermute(value, axis, [(i, (i + steps) % count) for i in range(count)])


def fetched(value, axis, steps):
    return moved(value, axis, -steps)


def swapped(value):
    return moved(value, "core", 1)


def transposed(value):
    rows, columns = lax.axis_size("dp"), lax.axis_size("y")
    pairs = [(x * columns + y, y * columns + x) for x in range(rows) for y in range(columns)]
    return lax.ppermute(value, ("dp", "y"), pairs)


def place_kernel(first, second, group, *refs):
    own, plus, two_a, two_b, minus = refs[:5]
    outs = refs[5 : 5 + group]
    sems = refs[5 + group]
    count = 4
    f = lax.axis_index(first)
    s = lax.axis_index(second)
    copies = []
    for e in range(count):
        for d in range(count):
            if e == 0:
                source = own.at[d]
            elif e == 1:
                source = plus.at[d]
            elif e == 3:
                source = minus.at[d]
            elif d < 2:
                source = two_a.at[d]
            else:
                source = two_b.at[d - 2]
            f_at = lax.rem(f + d, count)
            s_at = lax.rem(s + e, count)
            chip = f_at * count + s_at if first == "dp" else s_at * count + f_at
            for g in range(group):
                copies.append(
                    pltpu.make_async_copy(source.at[g], outs[g].at[chip], sems.at[len(copies)])
                )
    for copy in copies:
        copy.start()
    for copy in copies:
        copy.wait()


def split_at(columns):
    return columns // 256 * 128


class Gather:
    def __init__(self, shards, first, second):
        self.first, self.second, self.group = first, second, len(shards)
        self.shard = jnp.stack(shards)

    def neighbours(self, earlier=None):
        shard = after(self.shard, earlier)
        self.near = fetched(shard, self.first, 1), fetched(shard, self.first, 3)
        return self.near

    def along_first(self):
        plus, minus = self.near
        half = split_at(plus.shape[-1])
        two_a = fetched(plus[..., :half], self.first, 1)
        two_b = fetched(minus[..., half:], self.first, 3)
        two = jnp.concatenate([two_a, two_b], axis=-1)
        self.bundle = jnp.stack([self.shard, plus, two, minus])
        return self.bundle

    def along_second(self, earlier=None):
        bundle = after(self.bundle, earlier)
        self.plus = fetched(bundle, self.second, 1)
        self.minus = fetched(bundle, self.second, 3)
        return self.plus, self.minus

    def placed(self):
        two_a = fetched(self.plus[:2], self.second, 1)
        two_b = fetched(self.minus[2:], self.second, 3)
        rows, columns = self.shard.shape[1:]
        wholes = pl.pallas_call(
            functools.partial(place_kernel, self.first, self.second, self.group),
            out_shape=[jax.ShapeDtypeStruct((16, rows, columns), self.shard.dtype)] * self.group,
            in_specs=[pl.BlockSpec(memory_space=pltpu.VMEM)] * 5,
            out_specs=[pl.BlockSpec(memory_space=pl.ANY)] * self.group,
            scratch_shapes=[pltpu.SemaphoreType.DMA((16 * self.group,))],
            compiler_params=pltpu.CompilerParams(vmem_limit_bytes=VMEM_LIMIT),
            name="place_" + self.first,
        )(self.bundle, self.plus, two_a, two_b, self.minus)
        return [whole.reshape(16 * rows, columns) for whole in wholes]


def gathered_vectors(vectors):
    count, width = vectors.shape
    own = jnp.pad(vectors, ((0, 8 - count), (0, 128 - width)))
    other = swapped(own)
    core_zero = lax.axis_index("core") == 0
    block = jnp.stack([picked(core_zero, own, other), picked(core_zero, other, own)])
    rows = jnp.stack([block] + [fetched(block, "y", d) for d in (1, 2, 3)])
    plane = jnp.stack([rows] + [fetched(rows, "dp", d) for d in (1, 2, 3)])
    plane = jnp.roll(plane, (lax.axis_index("dp"), lax.axis_index("y")), (0, 1))
    plane = plane[:, :, :, :count, :width].transpose(3, 0, 1, 2, 4)
    return plane.reshape(count, -1).astype(F32)


class Scatter:
    def __init__(self, wholes, big, small):
        self.big, self.small = big, small
        self.grids = [whole.reshape((4, 4, whole.shape[0] // 16, whole.shape[1])) for whole in wholes]
        self.along = 0 if big == "dp" else 1
        self.at_big = lax.axis_index(big)
        self.at_small = lax.axis_index(small)

    def chunk(self, steps, lower=0, upper=4):
        at = lax.rem(self.at_big + steps, 4)
        parts = []
        for grid in self.grids:
            part = lax.dynamic_index_in_dim(grid, at, self.along, keepdims=False)
            parts.append(part[lower:upper])
        return parts[0] if len(parts) == 1 else jnp.concatenate(parts, axis=-1)

    def far(self):
        self.far_right, self.far_left = self.chunk(2, 0, 2), self.chunk(2, 2, 4)
        return self.far_right, self.far_left

    def near(self, earlier=None):
        far_right, far_left = after((self.far_right, self.far_left), earlier)
        from_left = moved(far_right, self.big, 1)
        from_right = moved(far_left, self.big, -1)
        self.right = jnp.concatenate([added(self.chunk(1, 0, 2), from_left), self.chunk(1, 2, 4)])
        self.left = jnp.concatenate([self.chunk(3, 0, 2), added(self.chunk(3, 2, 4), from_right)])
        return self.right, self.left

    def bundle(self, earlier=None):
        right, left = after((self.right, self.left), earlier)
        got_left = moved(right, self.big, 1)
        got_right = moved(left, self.big, -1)
        mine = self.chunk(0).astype(F32) + got_left.astype(F32) + got_right.astype(F32)
        self.mine = mine.astype(BF)
        return self.mine

    def piece(self, steps):
        return lax.dynamic_index_in_dim(self.mine, lax.rem(self.at_small + steps, 4), 0, keepdims=False)

    def small_far(self):
        far = self.piece(2)
        half = split_at(far.shape[-1])
        from_left = moved(far[:, :half], self.small, 1)
        from_right = moved(far[:, half:], self.small, -1)
        right, left = self.piece(1), self.piece(3)
        self.right = jnp.concatenate([added(right[:, :half], from_left), right[:, half:]], axis=1)
        self.left = jnp.concatenate([left[:, :half], added(left[:, half:], from_right)], axis=1)
        return self.right, self.left

    def total(self, earlier=None):
        right, left = after((self.right, self.left), earlier)
        got_left = moved(right, self.small, 1)
        got_right = moved(left, self.small, -1)
        return self.piece(0).astype(F32) + got_left.astype(F32) + got_right.astype(F32)


def added(left, right):
    return (left.astype(F32) + right.astype(F32)).astype(BF)


def after(value, earlier):
    return value if earlier is None else lax.optimization_barrier((value, earlier))[0]


def picked(first, value_zero, value_one):
    return jnp.where(first, value_zero, value_one)


def norm_parts(values):
    centered = values - jnp.mean(values, axis=-1, keepdims=True)
    spread = jnp.mean(centered * centered, axis=-1, keepdims=True)
    scale = lax.rsqrt(spread + EPSILON)
    return centered * scale, scale


def layer_norm(values, gain, bias):
    return norm_parts(values)[0] * gain + bias


def layer_norm_back(values, gain, grad):
    unit, scale = norm_parts(values)
    inner = grad * gain
    mean_inner = jnp.mean(inner, axis=-1, keepdims=True)
    mean_cross = jnp.mean(inner * unit, axis=-1, keepdims=True)
    grad_in = scale * (inner - mean_inner - unit * mean_cross)
    return grad_in, unit


NT = (((1,), (1,)), ((), ()))
NN = (((1,), (0,)), ((), ()))


def mxu(left, right, dims=NN):
    return lax.dot_general(left, right, dims, preferred_element_type=F32)


def half_mask(shape, half, axis):
    places = lax.broadcasted_iota(jnp.int32, shape, axis)
    return (places < HEAD_DIM) if half == 0 else (places >= HEAD_DIM)


def whole():
    return pl.BlockSpec(memory_space=pltpu.VMEM)


def called(kernel, name, out_shape, operands, flops, transcendentals):
    shapes = [(o.shape, o.dtype) for o in (*operands, *out_shape)]
    return pl.pallas_call(
        kernel,
        out_shape=out_shape,
        in_specs=[whole()] * len(operands),
        out_specs=[whole()] * len(out_shape),
        compiler_params=pltpu.CompilerParams(vmem_limit_bytes=VMEM_LIMIT),
        cost_estimate=pl.CostEstimate(
            flops=flops,
            bytes_accessed=sum(math.prod(shape) * dtype.itemsize for shape, dtype in shapes),
            transcendentals=transcendentals,
        ),
        name=name,
    )(*operands)


def by_head(block):
    zero = jnp.zeros_like(block)
    return jnp.concatenate([jnp.where(half_mask(block.shape, h, 1), block, zero) for h in range(2)])


def of_heads(rows):
    half = rows.shape[0] // 2
    return jnp.where(half_mask((half, rows.shape[1]), 0, 1), rows[:half], rows[half:])


def attend_kernel(save, q_ref, kv_ref, mark_q_ref, mark_k_ref, out_ref, *kept):
    scaling = jnp.asarray(HEAD_DIM ** (-0.5), BF)
    mark_k = mark_k_ref[...]
    mark_q = jnp.concatenate([mark_q_ref[...]] * 2)
    queries = q_ref.shape[0]
    for pair in range(q_ref.shape[1] // 128):
        q = by_head(q_ref[:, 128 * pair : 128 * pair + 128] * scaling)
        k = kv_ref[:, 256 * pair : 256 * pair + 128]
        v = kv_ref[:, 256 * pair + 128 : 256 * pair + 256]
        q_marked = jnp.concatenate([q, mark_q], axis=1)
        k_marked = jnp.concatenate([k, mark_k], axis=1)
        scores = mxu(q_marked, k_marked, NT)
        top = jnp.max(scores, axis=1, keepdims=True)
        probs = jnp.exp(scores - top).astype(BF)
        out = mxu(probs, jnp.concatenate([v, jnp.ones_like(v)], axis=1))
        total = out[:, 128:]
        out_ref[:, 128 * pair : 128 * pair + 128] = of_heads(out[:, :128] / total).astype(BF)
        if save:
            lse = top + jnp.log(total[:, :1])
            kept[0][:, 2 * pair : 2 * pair + 1] = lse[:queries]
            kept[0][:, 2 * pair + 1 : 2 * pair + 2] = lse[queries:]


def attend(q, kv, mark_q, mark_k, save):
    queries, width = q.shape
    keys = kv.shape[0]
    out_shape = [jax.ShapeDtypeStruct((queries, width), BF)]
    if save:
        out_shape.append(jax.ShapeDtypeStruct((queries, width // HEAD_DIM), F32))
    flops, exps = 16 * queries * keys * width, 2 * queries * keys * width // 128
    return called(
        functools.partial(attend_kernel, save), "attend", out_shape, (q, kv, mark_q, mark_k), flops, exps
    )


def attend_back_kernel(q_ref, kv_ref, do_ref, out_ref, lse_ref, mark_q_ref, mark_k_ref, dq_ref, dkv_ref):
    scaling = jnp.asarray(HEAD_DIM ** (-0.5), BF)
    mark_k = mark_k_ref[...]
    mark_q = jnp.concatenate([mark_q_ref[...]] * 2)
    for pair in range(q_ref.shape[1] // 128):
        columns = slice(128 * pair, 128 * pair + 128)
        q = by_head(q_ref[:, columns] * scaling)
        do = by_head(do_ref[:, columns])
        out = by_head(out_ref[:, columns])
        k = kv_ref[:, 256 * pair : 256 * pair + 128]
        v = kv_ref[:, 256 * pair + 128 : 256 * pair + 256]
        lse = jnp.concatenate([lse_ref[:, 2 * pair : 2 * pair + 1], lse_ref[:, 2 * pair + 1 : 2 * pair + 2]])
        delta = jnp.sum(do.astype(F32) * out.astype(F32), axis=1, keepdims=True)
        q_marked = jnp.concatenate([q, mark_q], axis=1)
        k_marked = jnp.concatenate([k, mark_k], axis=1)
        probs = jnp.exp(mxu(q_marked, k_marked, NT) - lse)
        grad_scores = (probs * (mxu(do, v, NT) - delta)).astype(BF)
        dq_ref[:, columns] = (of_heads(mxu(grad_scores, k)) * HEAD_DIM ** (-0.5)).astype(BF)
        dkv_ref[:, 256 * pair : 256 * pair + 128] = mxu(q.T, grad_scores).T.astype(BF)
        dkv_ref[:, 256 * pair + 128 : 256 * pair + 256] = mxu(do.T, probs.astype(BF)).T.astype(BF)


def attend_back(q, kv, do, out, lse, mark_q, mark_k):
    queries, width = q.shape
    keys = kv.shape[0]
    out_shape = [jax.ShapeDtypeStruct(q.shape, BF), jax.ShapeDtypeStruct(kv.shape, BF)]
    flops, exps = 40 * queries * keys * width, 2 * queries * keys * width // 128
    operands = (q, kv, do, out, lse, mark_q, mark_k)
    return called(attend_back_kernel, "attend_back", out_shape, operands, flops, exps)


def gelu_and_slope(values):
    phi = 0.5 * (1.0 + lax.erf(values * 0.7071067811865476))
    slope = phi + values * (0.3989422804014327 * jnp.exp(-0.5 * values * values))
    return values * phi, slope


BLOCK = 256


def feed_kernel(save, x_ref, up, down, out_ref, act_ref, *kept):
    x = x_ref[...]
    for at in range(0, up.shape[1], BLOCK):
        columns = slice(at, at + BLOCK)
        act, slope = gelu_and_slope(mxu(x, up[:, columns]))
        act_ref[:, columns] = act.astype(BF)
        if save:
            kept[0][:, columns] = slope.astype(BF)
    for at in range(0, out_ref.shape[1], BLOCK):
        columns = slice(at, at + BLOCK)
        out_ref[:, columns] = mxu(act_ref[...], down[:, columns])


def feed(x, up, down, save):
    rows, width = x.shape
    units = up.shape[1]
    kept = jax.ShapeDtypeStruct((rows, units), BF)
    out_shape = [jax.ShapeDtypeStruct((rows, width), F32), kept] + ([kept] if save else [])
    flops, exps = 4 * rows * width * units, 2 * rows * units
    return called(functools.partial(feed_kernel, save), "feed", out_shape, (x, up, down), flops, exps)


def feed_back_kernel(g_ref, slope_ref, up, down, out_ref, grad_ref):
    g = g_ref[...]
    for at in range(0, down.shape[0], BLOCK):
        rows = slice(at, at + BLOCK)
        grad = mxu(g, down[rows, :], NT) * slope_ref[:, rows].astype(F32)
        grad_ref[:, rows] = grad.astype(BF)
    for at in range(0, out_ref.shape[1], BLOCK):
        rows = slice(at, at + BLOCK)
        out_ref[:, rows] = mxu(grad_ref[...], up[rows, :], NT)


def feed_back(g, slope, up, down):
    rows, width = g.shape
    units = up.shape[1]
    out_shape = [jax.ShapeDtypeStruct((rows, width), F32), jax.ShapeDtypeStruct((rows, units), BF)]
    return called(feed_back_kernel, "feed_back", out_shape, (g, slope, up, down), 4 * rows * width * units, 0)


def dot(left, right, dims=NN):
    return lax.dot_general(left, right, dims, preferred_element_type=F32)


def from_other(part):
    half = part.shape[0] // 2
    other = swapped(part.astype(BF)).astype(F32)
    return jnp.concatenate([other[half:], other[:half]])


class Forward:
    def __init__(self, start, ring, marks, norms, received=None):
        self.ring, self.marks, self.norms = ring, marks, norms
        self.start, self.received = start, received
        self.rows = start.shape[0]

    def norm(self, earlier=None):
        hidden_low = self.start
        if self.received is not None:
            received = after(self.received, earlier)
            hidden_low = jnp.where(lax.axis_index("section") == 0, self.start, received)
        self.hidden = hidden_low.astype(F32)
        self.hidden_other = swapped(hidden_low)
        normed = layer_norm(self.hidden, self.norms[0], self.norms[1]).astype(BF)
        self.normed = normed
        self.fetched = [fetched(normed, self.ring, d) for d in (1, 2, 3)]

    def collect(self, earlier=None):
        normed = self.normed
        ring_rows = jnp.concatenate(after([normed] + self.fetched, earlier))
        other_rows = swapped(ring_rows)
        self.normed_all = jnp.concatenate([ring_rows, other_rows])
        self.normed_chip = jnp.concatenate([normed, other_rows[: self.rows]])

    def attention(self, weights, save, earlier):
        normed_all, normed_chip = after((self.normed_all, self.normed_chip), earlier)
        self.kv = dot(normed_all, weights["kv"]).astype(BF)
        self.q = dot(normed_chip, weights["q"]).astype(BF)
        self.attended, *self.lse = attend(self.q, self.kv, *self.marks, save)

    def feed_forward(self, weights, save, arrivals):
        rows = self.rows
        part = dot(self.attended, weights["out"])
        hidden = jnp.concatenate([self.hidden, self.hidden_other.astype(F32)])
        self.middle = hidden + part + from_other(part)
        normed_ffn = layer_norm(self.middle, self.norms[2], self.norms[3]).astype(BF)
        self.normed_ffn = after(normed_ffn, arrivals)
        fed, self.act, *self.slope = feed(self.normed_ffn, *weights["feed"], save)
        self.fed = fed
        self.result = (self.middle[:rows] + fed[:rows] + swapped(fed[rows:].astype(BF)).astype(F32)).astype(BF)


class Backward:
    def __init__(self, grad_low, forward):
        self.grad_low, self.forward = grad_low, forward
        self.rows = grad_low.shape[0]
        self.grad_chip = jnp.concatenate([grad_low, swapped(grad_low)])

    def feed_forward(self, weights, earlier, arrivals):
        rows, forward = self.rows, self.forward
        grad_chip = after(self.grad_chip, earlier)
        back, self.grad_up = feed_back(grad_chip, *forward.slope, *weights["feed"])
        back = after(back, arrivals)
        grad_normed = back + from_other(back)
        gain = forward.norms[2]
        part, unit = layer_norm_back(forward.middle, gain, grad_normed)
        self.grad_gain_ffn = jnp.sum(grad_normed[:rows] * unit[:rows], axis=0)
        self.grad_bias_ffn = jnp.sum(grad_normed[:rows], axis=0)
        grad_middle = grad_chip.astype(F32) + part
        self.grad_middle = grad_middle[:rows]
        self.grad_middle_low = grad_middle.astype(BF)
        self.grad_heads = dot(self.grad_middle_low, weights["out"], NT).astype(BF)

    def attention(self, weights, earlier):
        forward = self.forward
        grad_heads = after(self.grad_heads, earlier)
        self.dq, self.dkv = attend_back(
            forward.q, forward.kv, grad_heads, forward.attended, *forward.lse, *forward.marks
        )

    def project(self, weights, earlier=None):
        rows = self.rows
        self.dq, self.dkv = after((self.dq, self.dkv), earlier)
        grad_all = dot(self.dkv, weights["kv"], NT)
        grad_chip = dot(self.dq, weights["q"], NT)
        half = grad_all.shape[0] // 2
        own = jnp.concatenate([grad_all[:rows] + grad_chip[:rows], grad_all[rows:half]])
        away = jnp.concatenate([grad_all[half : half + rows] + grad_chip[rows:], grad_all[half + rows :]])
        self.ring_grads = own + swapped(away.astype(BF)).astype(F32)

    def spread(self):
        rows = self.rows
        self.pieces = [
            moved(self.ring_grads[d * rows : (d + 1) * rows].astype(BF), self.forward.ring, d)
            for d in (1, 2, 3)
        ]

    def reduce(self, earlier=None):
        forward = self.forward
        grad_normed = self.ring_grads[: self.rows]
        for piece in after(self.pieces, earlier):
            grad_normed = grad_normed + piece.astype(F32)
        part, unit = layer_norm_back(forward.hidden, forward.norms[0], grad_normed)
        self.grad_gain_attn = jnp.sum(grad_normed * unit, axis=0)
        self.grad_bias_attn = jnp.sum(grad_normed, axis=0)
        self.grad_hidden_low = (self.grad_middle + part).astype(BF)

    def vectors(self):
        return jnp.stack([self.grad_gain_attn, self.grad_bias_attn, self.grad_gain_ffn, self.grad_bias_ffn])


def marks_of(lengths, place, rows, core):
    index = lax.iota(jnp.int32, 8 * rows)
    core_at = jnp.where(index < 4 * rows, core, 1 - core)
    chip_at = lax.rem(place + lax.rem(index // rows, 4), 4)
    positions = chip_at * (2 * rows) + core_at * rows + lax.rem(index, rows)
    cells = lengths.shape[0]
    bounds = jnp.cumsum(lengths)
    segments = jnp.sum((positions[:, None] >= bounds[None, :]).astype(jnp.int32), axis=1, keepdims=True)
    places = lax.broadcasted_iota(jnp.int32, (1, 128), 1)
    own = segments == places
    mark_q = jnp.where(own | (places >= cells), 0.0, MASKED).astype(BF)
    mark_k = own.astype(BF)
    return jnp.concatenate([mark_q[:rows], mark_q[4 * rows : 5 * rows]]), mark_k


def attention_shards(w_qkv, w_out, core_zero):
    width = w_out.shape[1]
    half = width // 2

    def arranged(core):
        pieces = []
        for pair in range(half // 128):
            at = half * core + 128 * pair
            pieces.append(w_qkv[:, width + at : width + at + 128])
            pieces.append(w_qkv[:, 2 * width + at : 2 * width + at + 128])
        pieces.append(w_qkv[:, half * core : half * core + half])
        pieces.append(w_out[:, half * core : half * core + half])
        return jnp.concatenate(pieces, axis=1)

    both = exchanged_in(arranged(0), arranged(1), core_zero)
    return both[:, :width], both[:, width:]


def exchanged_in(zero, one, core_zero):
    mine = picked(core_zero, zero, one)
    other = swapped(picked(core_zero, one, zero))
    return jnp.concatenate([picked(core_zero, mine, other), picked(core_zero, other, mine)])


def up_shard(w_up, core_zero):
    rows = w_up.shape[0]
    units = w_up.reshape(rows, 16, 2, w_up.shape[1] // 32)
    return exchanged_in(units[:, :, 0].reshape(rows, -1), units[:, :, 1].reshape(rows, -1), core_zero)


def out_rows(out_half, core_zero):
    half = out_half.shape[1]
    zero, one = out_half[:half], out_half[half:]
    mine = picked(core_zero, zero, one)
    other = swapped(picked(core_zero, one, zero))
    return jnp.concatenate([picked(core_zero, mine, other), picked(core_zero, other, mine)], axis=1)


TN = (((0,), (0,)), ((), ()))


def summed(lefts, rights):
    return dot(jnp.concatenate(lefts), jnp.concatenate(rights), TN)


def feed_grads(backs):
    forwards = [back.forward for back in backs]
    down = summed([f.act for f in forwards], [back.grad_chip for back in backs])
    up = summed([f.normed_ffn for f in forwards], [back.grad_up for back in backs])
    return up.astype(BF), down.astype(BF)


def out_grads(backs, core_zero):
    grads = summed([back.forward.attended for back in backs], [back.grad_middle_low for back in backs])
    grads = grads.astype(BF)
    half = grads.shape[0]
    zero, one = grads[:, :half], grads[:, half:]
    mine = picked(core_zero, zero, one)
    other = swapped(picked(core_zero, one, zero))
    return jnp.concatenate([picked(core_zero, mine, other), picked(core_zero, other, mine)])


def query_grads(backs):
    return summed([back.forward.normed_chip for back in backs], [back.dq for back in backs]).astype(BF)


def key_value_grads(backs):
    return summed([back.forward.normed_all for back in backs], [back.dkv for back in backs]).astype(BF)


def vector_grads(backs):
    vectors = sum(back.vectors() for back in backs)
    vectors = jnp.pad(vectors, ((0, 128 - vectors.shape[0]), (0, 0))).astype(BF)
    vectors = vectors.astype(F32) + swapped(vectors).astype(F32)
    return vectors.astype(BF).T


def exchanged_out(shard, core_zero):
    rows = shard.shape[0] // 2
    zero, one = shard[:rows], shard[rows:]
    mine = picked(core_zero, zero, one)
    other = swapped(picked(core_zero, one, zero).astype(BF)).astype(F32)
    return picked(core_zero, mine, other), picked(core_zero, other, mine)


def whole_features(shard, section, target):
    both = jnp.stack([shard[0], transposed(shard[1])])
    pieces = []
    for z in range(4):
        pieces.append(both if z == target else lax.ppermute(both, "section", [(z, target)]))
    return jnp.concatenate(pieces, axis=2)


def spread_features(both, section, source):
    width = both.shape[2] // 4
    total = None
    for z in range(4):
        piece = both[:, :, z * width : (z + 1) * width]
        if z == source:
            piece = jnp.where(section == source, piece, jnp.zeros_like(piece))
        else:
            piece = lax.ppermute(piece, "section", [(source, z)])
        total = piece if total is None else total + piece
    return jnp.stack([total[0], transposed(total[1])])


def local(
    block_input,
    cotangent,
    cell_lengths,
    norm_attn_gain,
    norm_attn_bias,
    w_qkv,
    w_out,
    norm_ffn_gain,
    norm_ffn_bias,
    w_up,
    w_down,
):
    section = lax.axis_index("section")
    at_x = lax.axis_index("dp")
    at_y = lax.axis_index("y")
    core = lax.axis_index("core")
    core_zero = core == 0
    sections = lax.axis_size("section")
    rows = block_input.shape[1]
    rings = ("y", "dp")
    width = w_out.shape[2]
    half = width // 2

    w_down_whole = lax.all_gather(w_down[0], ("dp", "y"), axis=0, tiled=True)
    w_up_whole = lax.all_gather(up_shard(w_up[0], core_zero), ("dp", "y"), axis=0, tiled=True)
    kv_shard, rest_shard = attention_shards(w_qkv[0], w_out[0], core_zero)
    kv, rest = Gather([kv_shard], "dp", "y"), Gather([rest_shard], "y", "dp")
    near = kv.neighbours() + rest.neighbours()
    vectors = jnp.concatenate([norm_attn_gain, norm_attn_bias, norm_ffn_gain, norm_ffn_bias])
    norms = gathered_vectors(after(vectors, near))
    norms = tuple(norms[i : i + 1] for i in range(4))
    start = whole_features(after(block_input, near), section, 0)
    kv.along_first()
    rest.along_first()
    kv.along_second()
    rest.along_second()
    passes = [Forward(start[m], rings[m], None, norms) for m in range(2)]
    for now in passes:
        now.norm()
    marks = (
        marks_of(cell_lengths[2 * at_x], at_y, rows, core),
        marks_of(cell_lengths[2 * at_y + 1], at_x, rows, core),
    )
    for m, now in enumerate(passes):
        now.marks = marks[m]
        now.collect()
    (w_kv,) = kv.placed()
    (rest_whole,) = rest.placed()
    weights = {"kv": w_kv, "q": rest_whole[:, :half], "out": out_rows(rest_whole[:, half:], core_zero)}
    weights["feed"] = (w_up_whole, w_down_whole)

    forward_pairs = [(s, s + 1) for s in range(sections - 1)]
    result = None
    for step in range(sections):
        final = step == sections - 1
        for m in range(2):
            now, other = passes[m], passes[1 - m]
            waiting = step + m > 0 and not (final and m == 1)
            now.attention(weights, final, result)
            if waiting:
                other.norm(now.attended)
            now.feed_forward(weights, final, other.fetched[::2] if waiting else None)
            if waiting:
                other.collect(now.fed)
            result = now.result
            if not final:
                received = lax.ppermute(result, "section", forward_pairs)
                passes[m] = Forward(start[m], rings[m], marks[m], norms, received)
    block_output = spread_features(jnp.stack([now.result for now in passes]), section, sections - 1)

    last_grad = whole_features(cotangent, section, sections - 1)
    backs = [Backward(last_grad[m], passes[m]) for m in range(2)]
    backward_pairs = [(s + 1, s) for s in range(sections - 1)]
    earlier = result
    for step in range(sections):
        final = step == sections - 1
        for m in range(2):
            now, other = backs[m], backs[1 - m]
            waiting = step + m > 0
            now.feed_forward(weights, earlier, other.pieces[::2] if waiting else None)
            if waiting:
                other.reduce(now.grad_heads)
            if final and m == 1:
                break
            now.attention(weights, other.grad_hidden_low if waiting else None)
            if waiting:
                received = lax.ppermute(other.grad_hidden_low, "section", backward_pairs)
                received = after(received, now.dkv)
                grad_low = jnp.where(section == sections - 1, last_grad[1 - m], received)
                now.project(weights, grad_low)
                backs[1 - m] = Backward(grad_low, passes[1 - m])
            else:
                now.project(weights)
            now.spread()
            earlier = now.ring_grads

    arrived = backs[0].pieces
    up_grad, down_grad = feed_grads(backs)
    up_grads = lax.psum_scatter(up_grad, ("dp", "y"), scatter_dimension=0, tiled=True)
    sum_zero = Scatter([after(down_grad[:, :half], arrived)], "y", "dp")
    sum_one = Scatter([after(down_grad[:, half:], arrived)], "dp", "y")
    far = sum_zero.far() + sum_one.far()
    backs[1].attention(weights, (backs[0].grad_hidden_low, far))
    near = sum_zero.near() + sum_one.near()
    backs[1].project(weights, near)
    backs[1].spread()
    mine = sum_zero.bundle(), sum_one.bundle()
    sum_kv = Scatter([key_value_grads(backs)], "y", "dp")
    out_part = out_grads(backs, core_zero)
    query_part = query_grads(backs)
    backs[1].reduce(mine)
    sum_rest = Scatter([query_part, out_part, vector_grads(backs)], "dp", "y")
    sum_kv.far()
    sum_rest.far()
    near = sum_kv.near(mine) + sum_rest.near(mine)
    sum_zero.small_far()
    sum_one.small_far()
    mine = sum_kv.bundle(), sum_rest.bundle()
    down_grads = [sum_zero.total(near), sum_one.total(near)]
    input_grad = spread_features(
        after(jnp.stack([now.grad_hidden_low for now in backs]), near), section, 0
    ).astype(F32)
    sum_kv.small_far()
    sum_rest.small_far()
    kv_grads = sum_kv.total()
    rest_grads = sum_rest.total()

    own_rows = w_out.shape[1]
    units = jnp.stack(exchanged_out(up_grads.astype(F32), core_zero), axis=1)
    units = units.reshape(own_rows, 2, 16, -1).transpose(0, 2, 1, 3)
    grad_up = units.reshape(own_rows, -1)
    grad_down = jnp.concatenate(down_grads, axis=1)
    kv_cores = exchanged_out(kv_grads, core_zero)
    rest_cores = exchanged_out(rest_grads[:, :width], core_zero)
    keys, values = [], []
    for part in kv_cores:
        for pair in range(half // 128):
            keys.append(part[:, 256 * pair : 256 * pair + 128])
            values.append(part[:, 256 * pair + 128 : 256 * pair + 256])
    grad_qkv = jnp.concatenate([rest_cores[0][:, :half], rest_cores[1][:, :half]] + keys + values, axis=1)
    grad_out = jnp.concatenate([rest_cores[0][:, half:width], rest_cores[1][:, half:width]], axis=1)
    columns = rest_grads[:, width:]
    grad_vectors = picked(core_zero, columns[:own_rows], columns[own_rows:]).T[:4]
    return (
        block_output,
        input_grad,
        grad_vectors[0:1],
        grad_vectors[1:2],
        grad_qkv[None],
        grad_out[None],
        grad_vectors[2:3],
        grad_vectors[3:4],
        grad_up[None],
        grad_down[None],
    )


def solution(mesh):
    sizes = mesh.devices.shape
    cores = Mesh(mesh.devices.reshape(sizes[0], sizes[1], sizes[2] // 2, 2), ("section", "dp", "y", "core"))
    seq = ("y", "core")
    plane = ("dp", "y", "core")
    rows = P("dp", seq, "section")
    vector = P("section", plane)
    matrix = P("section", plane, None)
    return jax.shard_map(
        local,
        mesh=cores,
        in_specs=(rows, rows, P(), vector, vector, matrix, matrix, vector, vector, matrix, matrix),
        out_specs=(rows, rows, vector, vector, matrix, matrix, vector, vector, matrix, matrix),
        check_vma=False,
    )
```

```python
import functools
import math

import jax
import jax.numpy as jnp
from jax import lax
from jax.experimental import pallas as pl
from jax.experimental.pallas import tpu as pltpu
from jax.sharding import Mesh, PartitionSpec as P

HEAD_DIM = 64
EPSILON = 1e-05
MASKED = -1e30
BF = jnp.bfloat16
F32 = jnp.float32
BLOCK = 256
VMEM_LIMIT = 20 * 1024 * 1024


def moved(value, axis, steps):
    count = lax.axis_size(axis)
    return lax.ppermute(value, axis, [(i, (i + steps) % count) for i in range(count)])


def fetched(value, axis, steps):
    return moved(value, axis, -steps)


def swapped(value):
    return moved(value, "core", 1)


def transposed(value):
    rows, columns = lax.axis_size("dp"), lax.axis_size("y")
    pairs = [(x * columns + y, y * columns + x) for x in range(rows) for y in range(columns)]
    return lax.ppermute(value, ("dp", "y"), pairs)


def place_kernel(first, second, group, *refs):
    own, plus, two_a, two_b, minus = refs[:5]
    outs = refs[5 : 5 + group]
    sems = refs[5 + group]
    count = 4
    f = lax.axis_index(first)
    s = lax.axis_index(second)
    copies = []
    for e in range(count):
        for d in range(count):
            if e == 0:
                source = own.at[d]
            elif e == 1:
                source = plus.at[d]
            elif e == 3:
                source = minus.at[d]
            elif d < 2:
                source = two_a.at[d]
            else:
                source = two_b.at[d - 2]
            f_at = lax.rem(f + d, count)
            s_at = lax.rem(s + e, count)
            chip = f_at * count + s_at if first == "dp" else s_at * count + f_at
            for g in range(group):
                copies.append(
                    pltpu.make_async_copy(source.at[g], outs[g].at[chip], sems.at[len(copies)])
                )
    for copy in copies:
        copy.start()
    for copy in copies:
        copy.wait()


def split_at(columns):
    return columns // 256 * 128


class Gather:
    def __init__(self, shards, first, second):
        self.first, self.second, self.group = first, second, len(shards)
        self.shard = jnp.stack(shards)

    def neighbours(self, earlier=None):
        shard = after(self.shard, earlier)
        self.near = fetched(shard, self.first, 1), fetched(shard, self.first, 3)
        return self.near

    def along_first(self):
        plus, minus = self.near
        half = split_at(plus.shape[-1])
        two_a = fetched(plus[..., :half], self.first, 1)
        two_b = fetched(minus[..., half:], self.first, 3)
        two = jnp.concatenate([two_a, two_b], axis=-1)
        self.bundle = jnp.stack([self.shard, plus, two, minus])
        return self.bundle

    def along_second(self, earlier=None):
        bundle = after(self.bundle, earlier)
        self.plus = fetched(bundle, self.second, 1)
        self.minus = fetched(bundle, self.second, 3)
        return self.plus, self.minus

    def placed(self):
        two_a = fetched(self.plus[:2], self.second, 1)
        two_b = fetched(self.minus[2:], self.second, 3)
        rows, columns = self.shard.shape[1:]
        wholes = pl.pallas_call(
            functools.partial(place_kernel, self.first, self.second, self.group),
            out_shape=[jax.ShapeDtypeStruct((16, rows, columns), self.shard.dtype)] * self.group,
            in_specs=[pl.BlockSpec(memory_space=pltpu.VMEM)] * 5,
            out_specs=[pl.BlockSpec(memory_space=pl.ANY)] * self.group,
            scratch_shapes=[pltpu.SemaphoreType.DMA((16 * self.group,))],
            compiler_params=pltpu.CompilerParams(vmem_limit_bytes=VMEM_LIMIT),
            name="place_" + self.first,
        )(self.bundle, self.plus, two_a, two_b, self.minus)
        return [whole.reshape(16 * rows, columns) for whole in wholes]


class Scatter:
    def __init__(self, wholes, big, small):
        self.big, self.small = big, small
        self.grids = [whole.reshape((4, 4, whole.shape[0] // 16, whole.shape[1])) for whole in wholes]
        self.along = 0 if big == "dp" else 1
        self.at_big = lax.axis_index(big)
        self.at_small = lax.axis_index(small)

    def chunk(self, steps, lower=0, upper=4):
        at = lax.rem(self.at_big + steps, 4)
        parts = []
        for grid in self.grids:
            part = lax.dynamic_index_in_dim(grid, at, self.along, keepdims=False)
            parts.append(part[lower:upper])
        return parts[0] if len(parts) == 1 else jnp.concatenate(parts, axis=-1)

    def far(self):
        self.far_right, self.far_left = self.chunk(2, 0, 2), self.chunk(2, 2, 4)
        return self.far_right, self.far_left

    def near(self, earlier=None):
        far_right, far_left = after((self.far_right, self.far_left), earlier)
        from_left = moved(far_right, self.big, 1)
        from_right = moved(far_left, self.big, -1)
        self.right = jnp.concatenate([added(self.chunk(1, 0, 2), from_left), self.chunk(1, 2, 4)])
        self.left = jnp.concatenate([self.chunk(3, 0, 2), added(self.chunk(3, 2, 4), from_right)])
        return self.right, self.left

    def bundle(self, earlier=None):
        right, left = after((self.right, self.left), earlier)
        got_left = moved(right, self.big, 1)
        got_right = moved(left, self.big, -1)
        mine = self.chunk(0).astype(F32) + got_left.astype(F32) + got_right.astype(F32)
        self.mine = mine.astype(BF)
        return self.mine

    def piece(self, steps):
        return lax.dynamic_index_in_dim(self.mine, lax.rem(self.at_small + steps, 4), 0, keepdims=False)

    def small_far(self):
        far = self.piece(2)
        half = split_at(far.shape[-1])
        from_left = moved(far[:, :half], self.small, 1)
        from_right = moved(far[:, half:], self.small, -1)
        right, left = self.piece(1), self.piece(3)
        self.right = jnp.concatenate([added(right[:, :half], from_left), right[:, half:]], axis=1)
        self.left = jnp.concatenate([left[:, :half], added(left[:, half:], from_right)], axis=1)
        return self.right, self.left

    def total(self, earlier=None):
        right, left = after((self.right, self.left), earlier)
        got_left = moved(right, self.small, 1)
        got_right = moved(left, self.small, -1)
        return self.piece(0).astype(F32) + got_left.astype(F32) + got_right.astype(F32)


def added(left, right):
    return (left.astype(F32) + right.astype(F32)).astype(BF)


def after(value, earlier):
    return value if earlier is None else lax.optimization_barrier((value, earlier))[0]


def picked(first, value_zero, value_one):
    return jnp.where(first, value_zero, value_one)


def norm_parts(values):
    centered = values - jnp.mean(values, axis=-1, keepdims=True)
    spread = jnp.mean(centered * centered, axis=-1, keepdims=True)
    scale = lax.rsqrt(spread + EPSILON)
    return centered * scale, scale


def layer_norm(values, gain, bias):
    return norm_parts(values)[0] * gain + bias


def layer_norm_back(values, gain, grad):
    unit, scale = norm_parts(values)
    inner = grad * gain
    mean_inner = jnp.mean(inner, axis=-1, keepdims=True)
    mean_cross = jnp.mean(inner * unit, axis=-1, keepdims=True)
    grad_in = scale * (inner - mean_inner - unit * mean_cross)
    return grad_in, unit


NT = (((1,), (1,)), ((), ()))
NN = (((1,), (0,)), ((), ()))


def mxu(left, right, dims=NN):
    return lax.dot_general(left, right, dims, preferred_element_type=F32)


def half_mask(shape, half, axis):
    places = lax.broadcasted_iota(jnp.int32, shape, axis)
    return (places < HEAD_DIM) if half == 0 else (places >= HEAD_DIM)


def whole():
    return pl.BlockSpec(memory_space=pltpu.VMEM)


def called(kernel, name, out_shape, operands, flops, transcendentals):
    shapes = [(o.shape, o.dtype) for o in (*operands, *out_shape)]
    return pl.pallas_call(
        kernel,
        out_shape=out_shape,
        in_specs=[whole()] * len(operands),
        out_specs=[whole()] * len(out_shape),
        compiler_params=pltpu.CompilerParams(vmem_limit_bytes=VMEM_LIMIT),
        cost_estimate=pl.CostEstimate(
            flops=flops,
            bytes_accessed=sum(math.prod(shape) * dtype.itemsize for shape, dtype in shapes),
            transcendentals=transcendentals,
        ),
        name=name,
    )(*operands)


def by_head(block):
    zero = jnp.zeros_like(block)
    return jnp.concatenate([jnp.where(half_mask(block.shape, h, 1), block, zero) for h in range(2)])


def of_heads(rows):
    half = rows.shape[0] // 2
    return jnp.where(half_mask((half, rows.shape[1]), 0, 1), rows[:half], rows[half:])


def attend_kernel(save, q_ref, kv_ref, mark_q_ref, mark_k_ref, out_ref, *kept):
    scaling = jnp.asarray(HEAD_DIM ** (-0.5), BF)
    mark_k = mark_k_ref[...]
    mark_q = jnp.concatenate([mark_q_ref[...]] * 2)
    queries = q_ref.shape[0]
    for pair in range(q_ref.shape[1] // 128):
        q = by_head(q_ref[:, 128 * pair : 128 * pair + 128] * scaling)
        k = kv_ref[:, 256 * pair : 256 * pair + 128]
        v = kv_ref[:, 256 * pair + 128 : 256 * pair + 256]
        q_marked = jnp.concatenate([q, mark_q], axis=1)
        k_marked = jnp.concatenate([k, mark_k], axis=1)
        scores = mxu(q_marked, k_marked, NT)
        top = jnp.max(scores, axis=1, keepdims=True)
        probs = jnp.exp(scores - top).astype(BF)
        out = mxu(probs, jnp.concatenate([v, jnp.ones_like(v)], axis=1))
        total = out[:, 128:]
        out_ref[:, 128 * pair : 128 * pair + 128] = of_heads(out[:, :128] / total).astype(BF)
        if save:
            lse = top + jnp.log(total[:, :1])
            kept[0][:, 2 * pair : 2 * pair + 1] = lse[:queries]
            kept[0][:, 2 * pair + 1 : 2 * pair + 2] = lse[queries:]


def attend(q, kv, mark_q, mark_k, save):
    queries, width = q.shape
    keys = kv.shape[0]
    out_shape = [jax.ShapeDtypeStruct((queries, width), BF)]
    if save:
        out_shape.append(jax.ShapeDtypeStruct((queries, width // HEAD_DIM), F32))
    flops, exps = 16 * queries * keys * width, 2 * queries * keys * width // 128
    return called(
        functools.partial(attend_kernel, save), "attend", out_shape, (q, kv, mark_q, mark_k), flops, exps
    )


def attend_back_kernel(q_ref, kv_ref, do_ref, out_ref, lse_ref, mark_q_ref, mark_k_ref, dq_ref, dkv_ref):
    scaling = jnp.asarray(HEAD_DIM ** (-0.5), BF)
    mark_k = mark_k_ref[...]
    mark_q = jnp.concatenate([mark_q_ref[...]] * 2)
    for pair in range(q_ref.shape[1] // 128):
        columns = slice(128 * pair, 128 * pair + 128)
        q = by_head(q_ref[:, columns] * scaling)
        do = by_head(do_ref[:, columns])
        out = by_head(out_ref[:, columns])
        k = kv_ref[:, 256 * pair : 256 * pair + 128]
        v = kv_ref[:, 256 * pair + 128 : 256 * pair + 256]
        lse = jnp.concatenate([lse_ref[:, 2 * pair : 2 * pair + 1], lse_ref[:, 2 * pair + 1 : 2 * pair + 2]])
        delta = jnp.sum(do.astype(F32) * out.astype(F32), axis=1, keepdims=True)
        q_marked = jnp.concatenate([q, mark_q], axis=1)
        k_marked = jnp.concatenate([k, mark_k], axis=1)
        probs = jnp.exp(mxu(q_marked, k_marked, NT) - lse)
        grad_scores = (probs * (mxu(do, v, NT) - delta)).astype(BF)
        dq_ref[:, columns] = (of_heads(mxu(grad_scores, k)) * HEAD_DIM ** (-0.5)).astype(BF)
        dkv_ref[:, 256 * pair : 256 * pair + 128] = mxu(q.T, grad_scores).T.astype(BF)
        dkv_ref[:, 256 * pair + 128 : 256 * pair + 256] = mxu(do.T, probs.astype(BF)).T.astype(BF)


def project_back_kernel(dq_ref, dkv_ref, w_q_ref, w_kv_ref, own_ref, away_ref):
    rows = dq_ref.shape[0] // 2
    half = dkv_ref.shape[0] // 2
    for at in range(0, own_ref.shape[1], BLOCK):
        columns = slice(at, at + BLOCK)
        by_kv = mxu(dkv_ref[...], w_kv_ref[columns, :], NT)
        by_q = mxu(dq_ref[...], w_q_ref[columns, :], NT)
        own_ref[:rows, columns] = by_kv[:rows] + by_q[:rows]
        own_ref[rows:, columns] = by_kv[rows:half]
        away_ref[:rows, columns] = (by_kv[half : half + rows] + by_q[rows:]).astype(BF)
        away_ref[rows:, columns] = by_kv[half + rows :].astype(BF)


def project_back(dq, dkv, w_q, w_kv):
    keys, width = dkv.shape
    out_shape = [jax.ShapeDtypeStruct((keys // 2, width), kind) for kind in (F32, BF)]
    flops = 2 * keys * width * width
    return called(project_back_kernel, "project_back", out_shape, (dq, dkv, w_q, w_kv), flops, 0)


def attend_back(q, kv, do, out, lse, mark_q, mark_k):
    queries, width = q.shape
    keys = kv.shape[0]
    out_shape = [jax.ShapeDtypeStruct(q.shape, BF), jax.ShapeDtypeStruct(kv.shape, BF)]
    flops, exps = 40 * queries * keys * width, 2 * queries * keys * width // 128
    operands = (q, kv, do, out, lse, mark_q, mark_k)
    return called(attend_back_kernel, "attend_back", out_shape, operands, flops, exps)


def gelu_and_slope(values):
    phi = 0.5 * (1.0 + lax.erf(values * 0.7071067811865476))
    slope = phi + values * (0.3989422804014327 * jnp.exp(-0.5 * values * values))
    return values * phi, slope


def feed_kernel(save, x_ref, up, down, out_ref, act_ref, *kept):
    x = x_ref[...]
    for at in range(0, up.shape[1], BLOCK):
        columns = slice(at, at + BLOCK)
        act, slope = gelu_and_slope(mxu(x, up[:, columns]))
        act_ref[:, columns] = act.astype(BF)
        if save:
            kept[0][:, columns] = slope.astype(BF)
    for at in range(0, out_ref.shape[1], BLOCK):
        columns = slice(at, at + BLOCK)
        out_ref[:, columns] = mxu(act_ref[...], down[:, columns])


def feed(x, up, down, save):
    rows, width = x.shape
    units = up.shape[1]
    kept = jax.ShapeDtypeStruct((rows, units), BF)
    out_shape = [jax.ShapeDtypeStruct((rows, width), F32), kept] + ([kept] if save else [])
    flops, exps = 4 * rows * width * units, 2 * rows * units
    return called(functools.partial(feed_kernel, save), "feed", out_shape, (x, up, down), flops, exps)


def feed_back_kernel(g_ref, slope_ref, up, down, out_ref, grad_ref):
    g = g_ref[...]
    for at in range(0, down.shape[0], BLOCK):
        rows = slice(at, at + BLOCK)
        grad = mxu(g, down[rows, :], NT) * slope_ref[:, rows].astype(F32)
        grad_ref[:, rows] = grad.astype(BF)
    for at in range(0, out_ref.shape[1], BLOCK):
        rows = slice(at, at + BLOCK)
        out_ref[:, rows] = mxu(grad_ref[...], up[rows, :], NT)


def feed_back(g, slope, up, down):
    rows, width = g.shape
    units = up.shape[1]
    out_shape = [jax.ShapeDtypeStruct((rows, width), F32), jax.ShapeDtypeStruct((rows, units), BF)]
    return called(feed_back_kernel, "feed_back", out_shape, (g, slope, up, down), 4 * rows * width * units, 0)


def dot(left, right, dims=NN):
    return lax.dot_general(left, right, dims, preferred_element_type=F32)


def from_other(part):
    half = part.shape[0] // 2
    other = swapped(part.astype(BF)).astype(F32)
    return jnp.concatenate([other[half:], other[:half]])


class Forward:
    def __init__(self, start, ring, marks, norms, received=None):
        self.ring, self.marks, self.norms = ring, marks, norms
        self.start, self.received = start, received
        self.rows = start.shape[0]

    def norm(self, earlier=None):
        hidden_low = self.start
        if self.received is not None:
            received = after(self.received, earlier)
            hidden_low = jnp.where(lax.axis_index("section") == 0, self.start, received)
        self.hidden = hidden_low.astype(F32)
        self.hidden_other = swapped(hidden_low)
        normed = layer_norm(self.hidden, self.norms[0], self.norms[1]).astype(BF)
        self.normed = normed
        self.near = fetched(normed, self.ring, 1), fetched(normed, self.ring, 3)

    def fetch_raw(self, earlier):
        self.hidden_low = after(self.start, earlier)
        self.hidden_other = swapped(self.hidden_low)
        self.near = fetched(self.hidden_low, self.ring, 1), fetched(self.hidden_low, self.ring, 3)
        self.fetch_far()

    def collect_raw(self):
        self.hidden = self.hidden_low.astype(F32)
        plus, minus = self.near
        ring_rows = jnp.concatenate([self.hidden_low, plus, *self.far, minus])
        rows = jnp.concatenate([ring_rows, swapped(ring_rows)]).astype(F32)
        self.normed_all = layer_norm(rows, self.norms[0], self.norms[1]).astype(BF)
        half = 4 * self.rows
        self.normed_chip = jnp.concatenate(
            [self.normed_all[: self.rows], self.normed_all[half : half + self.rows]]
        )

    def swap_near(self):
        plus, minus = self.near
        self.other_near = swapped(jnp.concatenate([self.normed, plus, minus]))

    def fetch_far(self):
        plus, minus = self.near
        half = self.rows // 2
        self.far = fetched(plus[:half], self.ring, 1), fetched(minus[half:], self.ring, 3)

    def collect(self, earlier=None):
        rows, normed = self.rows, self.normed
        plus, minus = self.near
        two = jnp.concatenate(after(self.far, earlier))
        other_near, other_two = self.other_near, swapped(two)
        self.normed_all = jnp.concatenate(
            [normed, plus, two, minus, other_near[: 2 * rows], other_two, other_near[2 * rows :]]
        )
        self.normed_chip = jnp.concatenate([normed, other_near[:rows]])

    def project(self, weights, earlier):
        normed_all, normed_chip = after((self.normed_all, self.normed_chip), earlier)
        self.kv = dot(normed_all, weights["kv"]).astype(BF)
        self.q = dot(normed_chip, weights["q"]).astype(BF)

    def attention(self, save):
        self.attended, *self.lse = attend(self.q, self.kv, *self.marks, save)

    def feed_forward(self, weights, save, arrivals, between):
        rows = self.rows
        part = dot(self.attended, weights["out"])
        hidden = jnp.concatenate([self.hidden, self.hidden_other.astype(F32)])
        self.middle = hidden + part + from_other(part)
        normed_ffn = layer_norm(self.middle, self.norms[2], self.norms[3]).astype(BF)
        self.normed_ffn = after(normed_ffn, arrivals)
        fed, self.act, *self.slope = feed(self.normed_ffn, *weights["feed"], save)
        self.fed = fed = after(fed, between)
        self.result = (self.middle[:rows] + fed[:rows] + swapped(fed[rows:].astype(BF)).astype(F32)).astype(BF)


class Backward:
    def __init__(self, grad_low, forward):
        self.grad_low, self.forward = grad_low, forward
        self.rows = grad_low.shape[0]
        self.grad_chip = jnp.concatenate([grad_low, swapped(grad_low)])

    def feed_forward(self, weights, earlier, arrivals):
        rows, forward = self.rows, self.forward
        grad_chip = after(self.grad_chip, earlier)
        back, self.grad_up = feed_back(grad_chip, *forward.slope, *weights["feed"])
        back = after(back, arrivals)
        grad_normed = back + from_other(back)
        gain = forward.norms[2]
        part, unit = layer_norm_back(forward.middle, gain, grad_normed)
        self.grad_gain_ffn = jnp.sum(grad_normed[:rows] * unit[:rows], axis=0)
        self.grad_bias_ffn = jnp.sum(grad_normed[:rows], axis=0)
        grad_middle = grad_chip.astype(F32) + part
        self.grad_middle = grad_middle[:rows]
        self.grad_middle_low = grad_middle.astype(BF)
        self.grad_heads = dot(self.grad_middle_low, weights["out"], NT).astype(BF)

    def attention(self, earlier):
        forward = self.forward
        grad_heads = after(self.grad_heads, earlier)
        self.dq, self.dkv = attend_back(
            forward.q, forward.kv, grad_heads, forward.attended, *forward.lse, *forward.marks
        )

    def project(self, weights, earlier=None):
        dq, dkv = after((self.dq, self.dkv), earlier)
        self.own, self.away = project_back(dq, dkv, weights["q"], weights["kv"])

    def sum_cores(self, earlier=None):
        rows = self.rows
        own, away = after((self.own, self.away), earlier)
        far = swapped(away[2 * rows : 3 * rows])
        near = swapped(jnp.concatenate([away[: 2 * rows], away[3 * rows :]]))
        self.ring_grads = [
            own[d * rows : (d + 1) * rows] + part.astype(F32)
            for d, part in enumerate((near[:rows], near[rows : 2 * rows], far, near[2 * rows :]))
        ]

    def piece(self, steps, lower=0, upper=None):
        return self.ring_grads[steps][lower : self.rows if upper is None else upper]

    def spread_far(self):
        half, ring = self.rows // 2, self.forward.ring
        self.far = (
            moved(self.piece(2, 0, half).astype(BF), ring, 1),
            moved(self.piece(2, half).astype(BF), ring, -1),
        )

    def spread_near(self, earlier=None):
        half, ring = self.rows // 2, self.forward.ring
        from_left, from_right = after(self.far, earlier)
        right = jnp.concatenate([self.piece(1, 0, half) + from_left.astype(F32), self.piece(1, half)])
        left = jnp.concatenate([self.piece(3, 0, half), self.piece(3, half) + from_right.astype(F32)])
        self.near = moved(right.astype(BF), ring, 1), moved(left.astype(BF), ring, -1)

    def reduce(self, earlier=None):
        forward = self.forward
        grad_normed = self.piece(0)
        for part in after(self.near, earlier):
            grad_normed = grad_normed + part.astype(F32)
        part, unit = layer_norm_back(forward.hidden, forward.norms[0], grad_normed)
        self.grad_gain_attn = jnp.sum(grad_normed * unit, axis=0)
        self.grad_bias_attn = jnp.sum(grad_normed, axis=0)
        self.grad_hidden_low = (self.grad_middle + part).astype(BF)

    def vectors(self):
        return jnp.stack([self.grad_gain_attn, self.grad_bias_attn, self.grad_gain_ffn, self.grad_bias_ffn])


def marks_of(lengths, place, rows, core):
    index = lax.iota(jnp.int32, 8 * rows)
    core_at = jnp.where(index < 4 * rows, core, 1 - core)
    chip_at = lax.rem(place + lax.rem(index // rows, 4), 4)
    positions = chip_at * (2 * rows) + core_at * rows + lax.rem(index, rows)
    cells = lengths.shape[0]
    bounds = jnp.cumsum(lengths)
    segments = jnp.sum((positions[:, None] >= bounds[None, :]).astype(jnp.int32), axis=1, keepdims=True)
    places = lax.broadcasted_iota(jnp.int32, (1, 128), 1)
    own = segments == places
    mark_q = jnp.where(own | (places >= cells), 0.0, MASKED).astype(BF)
    mark_k = own.astype(BF)
    return jnp.concatenate([mark_q[:rows], mark_q[4 * rows : 5 * rows]]), mark_k


def attention_shards(w_qkv, w_out, vectors, core_zero):
    width = w_out.shape[1]
    half = width // 2

    def arranged(core):
        pieces = []
        for pair in range(half // 128):
            at = half * core + 128 * pair
            pieces.append(w_qkv[:, width + at : width + at + 128])
            pieces.append(w_qkv[:, 2 * width + at : 2 * width + at + 128])
        pieces.append(w_qkv[:, half * core : half * core + half])
        pieces.append(w_out[:, half * core : half * core + half])
        pieces.append(jnp.pad(vectors.T, ((0, 0), (0, 128 - vectors.shape[0]))))
        return jnp.concatenate(pieces, axis=1)

    both = exchanged_in(arranged(0), arranged(1), core_zero)
    return both[:, :width], both[:, width:]


def exchanged_in(zero, one, core_zero):
    mine = picked(core_zero, zero, one)
    other = swapped(picked(core_zero, one, zero))
    return jnp.concatenate([picked(core_zero, mine, other), picked(core_zero, other, mine)])


def up_shard(w_up, core_zero):
    rows = w_up.shape[0]
    units = w_up.reshape(rows, 16, 2, w_up.shape[1] // 32)
    return exchanged_in(units[:, :, 0].reshape(rows, -1), units[:, :, 1].reshape(rows, -1), core_zero)


def out_rows(out_half, core_zero):
    half = out_half.shape[1]
    zero, one = out_half[:half], out_half[half:]
    mine = picked(core_zero, zero, one)
    other = swapped(picked(core_zero, one, zero))
    return jnp.concatenate([picked(core_zero, mine, other), picked(core_zero, other, mine)], axis=1)


TN = (((0,), (0,)), ((), ()))


def summed(lefts, rights):
    return dot(jnp.concatenate(lefts), jnp.concatenate(rights), TN)


def feed_grads(backs):
    forwards = [back.forward for back in backs]
    down = summed([f.act for f in forwards], [back.grad_chip for back in backs]).astype(BF)
    up = summed([f.normed_ffn for f in forwards], [back.grad_up for back in backs]).astype(BF)
    down = down.reshape(16, 2, -1, down.shape[1]).transpose(1, 0, 2, 3).reshape(2, -1, down.shape[1])
    return jnp.concatenate([up, down[0], down[1]], axis=1)


def out_grads(backs, core_zero):
    grads = summed([back.forward.attended for back in backs], [back.grad_middle_low for back in backs])
    grads = grads.astype(BF)
    half = grads.shape[0]
    zero, one = grads[:, :half], grads[:, half:]
    mine = picked(core_zero, zero, one)
    other = swapped(picked(core_zero, one, zero))
    return jnp.concatenate([picked(core_zero, mine, other), picked(core_zero, other, mine)])


def query_grads(backs):
    return summed([back.forward.normed_chip for back in backs], [back.dq for back in backs]).astype(BF)


def key_value_grads(backs, earlier):
    dkv = after([back.dkv for back in backs], earlier)
    return summed([back.forward.normed_all for back in backs], dkv).astype(BF)


def vector_grads(backs):
    vectors = sum(back.vectors() for back in backs)
    vectors = jnp.pad(vectors, ((0, 128 - vectors.shape[0]), (0, 0))).astype(BF)
    return added(vectors, swapped(vectors)).T


def exchanged_out(shard, core_zero):
    rows = shard.shape[0] // 2
    zero, one = shard[:rows], shard[rows:]
    mine = picked(core_zero, zero, one)
    other = swapped(picked(core_zero, one, zero).astype(BF)).astype(F32)
    return picked(core_zero, mine, other), picked(core_zero, other, mine)


def whole_features(shard, section, target):
    both = jnp.stack([shard[0], transposed(shard[1])])
    pieces = []
    for z in range(4):
        pieces.append(both if z == target else lax.ppermute(both, "section", [(z, target)]))
    return jnp.concatenate(pieces, axis=2)


def spread_features(both, section, source):
    width = both.shape[2] // 4
    total = None
    for z in range(4):
        piece = both[:, :, z * width : (z + 1) * width]
        if z == source:
            piece = jnp.where(section == source, piece, jnp.zeros_like(piece))
        else:
            piece = lax.ppermute(piece, "section", [(source, z)])
        total = piece if total is None else total + piece
    return jnp.stack([total[0], transposed(total[1])])


def local(
    block_input,
    cotangent,
    cell_lengths,
    norm_attn_gain,
    norm_attn_bias,
    w_qkv,
    w_out,
    norm_ffn_gain,
    norm_ffn_bias,
    w_up,
    w_down,
):
    section = lax.axis_index("section")
    at_x = lax.axis_index("dp")
    at_y = lax.axis_index("y")
    core = lax.axis_index("core")
    core_zero = core == 0
    sections = lax.axis_size("section")
    rows = block_input.shape[1]
    rings = ("y", "dp")
    width = w_out.shape[2]
    half = width // 2

    w_down_whole = lax.all_gather(w_down[0], ("dp", "y"), axis=0, tiled=True)
    w_up_whole = lax.all_gather(up_shard(w_up[0], core_zero), ("dp", "y"), axis=0, tiled=True)
    vectors = jnp.concatenate([norm_attn_gain, norm_attn_bias, norm_ffn_gain, norm_ffn_bias])
    kv_shard, rest_shard = attention_shards(w_qkv[0], w_out[0], vectors, core_zero)
    kv, rest = Gather([kv_shard], "dp", "y"), Gather([rest_shard], "y", "dp")
    start = whole_features(block_input, section, 0)
    passes = [Forward(start[m], rings[m], None, None) for m in range(2)]
    near = kv.neighbours() + rest.neighbours()
    for now in passes:
        now.fetch_raw(near)
    kv.along_first()
    rest.along_first()
    kv.along_second()
    rest.along_second()
    marks = (
        marks_of(cell_lengths[2 * at_x], at_y, rows, core),
        marks_of(cell_lengths[2 * at_y + 1], at_x, rows, core),
    )
    (w_kv,) = kv.placed()
    (rest_whole,) = rest.placed()
    weights = {"kv": w_kv, "q": rest_whole[:, :half], "out": out_rows(rest_whole[:, half:width], core_zero)}
    norms = rest_whole[:, width:].T[:4].astype(F32)
    norms = tuple(norms[i : i + 1] for i in range(4))
    last_grad = whole_features(after(cotangent, (w_kv, rest_whole)), section, sections - 1)
    for m, now in enumerate(passes):
        now.marks, now.norms = marks[m], norms
        now.collect_raw()
    weights["feed"] = (w_up_whole, w_down_whole)

    forward_pairs = [(s, s + 1) for s in range(sections - 1)]
    result = None
    for step in range(sections):
        final = step == sections - 1
        for m in range(2):
            now, other = passes[m], passes[1 - m]
            waiting = step + m > 0 and not (final and m == 1)
            now.project(weights, result)
            now.attention(final)
            if waiting:
                other.norm(now.attended)
                now.attended = after(now.attended, other.normed)
                other.swap_near()
                other.fetch_far()
            now.feed_forward(
                weights, final, other.near if waiting else last_grad, other.other_near if waiting else None
            )
            if waiting:
                other.collect(now.fed)
            result = now.result
            if not final:
                received = lax.ppermute(result, "section", forward_pairs)
                passes[m] = Forward(start[m], rings[m], marks[m], norms, received)
    block_output = spread_features(jnp.stack([now.result for now in passes]), section, sections - 1)

    backs = [Backward(last_grad[m], passes[m]) for m in range(2)]
    backward_pairs = [(s + 1, s) for s in range(sections - 1)]
    earlier = result
    for step in range(sections):
        final = step == sections - 1
        for m in range(2):
            now, other = backs[m], backs[1 - m]
            waiting = step + m > 0
            if step == 1 and m == 0:
                earlier = (earlier, block_output)
            now.feed_forward(weights, earlier, other.far if waiting else None)
            if waiting:
                other.spread_near()
            if final and m == 1:
                break
            now.attention(None)
            if waiting:
                other.reduce(now.dkv)
                now.project(weights, other.grad_hidden_low)
                received = lax.ppermute(other.grad_hidden_low, "section", backward_pairs)
                received = after(received, now.own)
                grad_low = jnp.where(section == sections - 1, last_grad[1 - m], received)
                backs[1 - m] = Backward(grad_low, passes[1 - m])
                now.sum_cores(grad_low)
            else:
                now.project(weights)
                now.sum_cores()
            now.spread_far()
            earlier = now.ring_grads

    joint = feed_grads(backs)
    backs[0].reduce()
    backs[1].attention((backs[0].grad_hidden_low, joint))
    joint = lax.psum_scatter(joint, ("dp", "y"), scatter_dimension=0, tiled=True).astype(F32)
    backs[1].project(weights)
    backs[1].sum_cores()
    backs[1].spread_far()
    backs[1].spread_near()
    kv_part = key_value_grads(backs, backs[1].far)
    out_part = out_grads(backs, core_zero)
    query_part = query_grads(backs)
    backs[1].reduce((kv_part, query_part))
    sum_kv = Scatter([after(kv_part, backs[1].near)], "y", "dp")
    sum_rest = Scatter([query_part, out_part, vector_grads(backs)], "dp", "y")
    sum_kv.far()
    sum_rest.far()
    sum_kv.near()
    sum_rest.near()
    mine = sum_kv.bundle()
    sum_rest.bundle()
    input_grad = spread_features(
        after(jnp.stack([now.grad_hidden_low for now in backs]), mine), section, 0
    ).astype(F32)
    sum_kv.small_far()
    sum_rest.small_far()
    kv_grads = sum_kv.total()
    rest_grads = sum_rest.total()
    up_grads = joint[:, : 2 * width]
    grad_down = jnp.concatenate([joint[:, 2 * width : 3 * width], joint[:, 3 * width :]])

    own_rows = w_out.shape[1]
    units = jnp.stack(exchanged_out(up_grads, core_zero), axis=1)
    units = units.reshape(own_rows, 2, 16, -1).transpose(0, 2, 1, 3)
    grad_up = units.reshape(own_rows, -1)
    kv_cores = exchanged_out(kv_grads, core_zero)
    rest_cores = exchanged_out(rest_grads[:, :width], core_zero)
    keys, values = [], []
    for part in kv_cores:
        for pair in range(half // 128):
            keys.append(part[:, 256 * pair : 256 * pair + 128])
            values.append(part[:, 256 * pair + 128 : 256 * pair + 256])
    grad_qkv = jnp.concatenate([rest_cores[0][:, :half], rest_cores[1][:, :half]] + keys + values, axis=1)
    grad_out = jnp.concatenate([rest_cores[0][:, half:width], rest_cores[1][:, half:width]], axis=1)
    columns = rest_grads[:, width:]
    grad_vectors = picked(core_zero, columns[:own_rows], columns[own_rows:]).T[:4]
    return (
        block_output,
        input_grad,
        grad_vectors[0:1],
        grad_vectors[1:2],
        grad_qkv[None],
        grad_out[None],
        grad_vectors[2:3],
        grad_vectors[3:4],
        grad_up[None],
        grad_down[None],
    )


def solution(mesh):
    sizes = mesh.devices.shape
    cores = Mesh(mesh.devices.reshape(sizes[0], sizes[1], sizes[2] // 2, 2), ("section", "dp", "y", "core"))
    seq = ("y", "core")
    plane = ("dp", "y", "core")
    rows = P("dp", seq, "section")
    vector = P("section", plane)
    matrix = P("section", plane, None)
    return jax.shard_map(
        local,
        mesh=cores,
        in_specs=(rows, rows, P(), vector, vector, matrix, matrix, vector, vector, matrix, matrix),
        out_specs=(rows, rows, vector, vector, matrix, matrix, vector, vector, matrix, matrix),
        check_vma=False,
    )
```

```python
import functools
import math

import jax
import jax.numpy as jnp
from jax import lax
from jax.experimental import pallas as pl
from jax.experimental.pallas import tpu as pltpu
from jax.sharding import Mesh, PartitionSpec as P

HEAD_DIM = 64
EPSILON = 1e-05
MASKED = -1e30
BF = jnp.bfloat16
F32 = jnp.float32
BLOCK = 256
VMEM_LIMIT = 20 * 1024 * 1024


def moved(value, axis, steps):
    count = lax.axis_size(axis)
    return lax.ppermute(value, axis, [(i, (i + steps) % count) for i in range(count)])


def fetched(value, axis, steps):
    return moved(value, axis, -steps)


def swapped(value):
    return moved(value, "core", 1)


def transposed(value):
    rows, columns = lax.axis_size("dp"), lax.axis_size("y")
    pairs = [(x * columns + y, y * columns + x) for x in range(rows) for y in range(columns)]
    return lax.ppermute(value, ("dp", "y"), pairs)


def place_kernel(first, second, group, *refs):
    own, plus, two_a, two_b, minus = refs[:5]
    outs = refs[5 : 5 + group]
    sems = refs[5 + group]
    count = 4
    f = lax.axis_index(first)
    s = lax.axis_index(second)
    copies = []
    for e in range(count):
        for d in range(count):
            if e == 0:
                source = own.at[d]
            elif e == 1:
                source = plus.at[d]
            elif e == 3:
                source = minus.at[d]
            elif d < 2:
                source = two_a.at[d]
            else:
                source = two_b.at[d - 2]
            f_at = lax.rem(f + d, count)
            s_at = lax.rem(s + e, count)
            chip = f_at * count + s_at if first == "dp" else s_at * count + f_at
            for g in range(group):
                copies.append(
                    pltpu.make_async_copy(source.at[g], outs[g].at[chip], sems.at[len(copies)])
                )
    for copy in copies:
        copy.start()
    for copy in copies:
        copy.wait()


def split_at(columns):
    return columns // 256 * 128


class Gather:
    def __init__(self, shards, first, second):
        self.first, self.second, self.group = first, second, len(shards)
        self.shard = jnp.stack(shards)

    def neighbours(self, earlier=None):
        shard = after(self.shard, earlier)
        self.near = fetched(shard, self.first, 1), fetched(shard, self.first, 3)
        return self.near

    def along_first(self):
        plus, minus = self.near
        half = split_at(plus.shape[-1])
        two_a = fetched(plus[..., :half], self.first, 1)
        two_b = fetched(minus[..., half:], self.first, 3)
        two = jnp.concatenate([two_a, two_b], axis=-1)
        self.bundle = jnp.stack([self.shard, plus, two, minus])
        return self.bundle

    def along_second(self, earlier=None):
        bundle = after(self.bundle, earlier)
        self.plus = fetched(bundle, self.second, 1)
        self.minus = fetched(bundle, self.second, 3)
        return self.plus, self.minus

    def placed(self):
        two_a = fetched(self.plus[:2], self.second, 1)
        two_b = fetched(self.minus[2:], self.second, 3)
        rows, columns = self.shard.shape[1:]
        wholes = pl.pallas_call(
            functools.partial(place_kernel, self.first, self.second, self.group),
            out_shape=[jax.ShapeDtypeStruct((16, rows, columns), self.shard.dtype)] * self.group,
            in_specs=[pl.BlockSpec(memory_space=pltpu.VMEM)] * 5,
            out_specs=[pl.BlockSpec(memory_space=pl.ANY)] * self.group,
            scratch_shapes=[pltpu.SemaphoreType.DMA((16 * self.group,))],
            compiler_params=pltpu.CompilerParams(vmem_limit_bytes=VMEM_LIMIT),
            name="place_" + self.first,
        )(self.bundle, self.plus, two_a, two_b, self.minus)
        return [whole.reshape(16 * rows, columns) for whole in wholes]


class Scatter:
    def __init__(self, wholes, big, small):
        self.big, self.small = big, small
        self.grids = [whole.reshape((4, 4, whole.shape[0] // 16, whole.shape[1])) for whole in wholes]
        self.along = 0 if big == "dp" else 1
        self.at_big = lax.axis_index(big)
        self.at_small = lax.axis_index(small)

    def chunk(self, steps, lower=0, upper=4):
        at = lax.rem(self.at_big + steps, 4)
        parts = []
        for grid in self.grids:
            part = lax.dynamic_index_in_dim(grid, at, self.along, keepdims=False)
            parts.append(part[lower:upper])
        return parts[0] if len(parts) == 1 else jnp.concatenate(parts, axis=-1)

    def far(self):
        self.far_right, self.far_left = self.chunk(2, 0, 2), self.chunk(2, 2, 4)
        return self.far_right, self.far_left

    def near(self, earlier=None):
        far_right, far_left = after((self.far_right, self.far_left), earlier)
        from_left = moved(far_right, self.big, 1)
        from_right = moved(far_left, self.big, -1)
        self.right = jnp.concatenate([added(self.chunk(1, 0, 2), from_left), self.chunk(1, 2, 4)])
        self.left = jnp.concatenate([self.chunk(3, 0, 2), added(self.chunk(3, 2, 4), from_right)])
        return self.right, self.left

    def bundle(self, earlier=None):
        right, left = after((self.right, self.left), earlier)
        got_left = moved(right, self.big, 1)
        got_right = moved(left, self.big, -1)
        mine = self.chunk(0).astype(F32) + got_left.astype(F32) + got_right.astype(F32)
        self.mine = mine.astype(BF)
        return self.mine

    def piece(self, steps):
        return lax.dynamic_index_in_dim(self.mine, lax.rem(self.at_small + steps, 4), 0, keepdims=False)

    def small_far(self):
        far = self.piece(2)
        half = split_at(far.shape[-1])
        from_left = moved(far[:, :half], self.small, 1)
        from_right = moved(far[:, half:], self.small, -1)
        right, left = self.piece(1), self.piece(3)
        self.right = jnp.concatenate([added(right[:, :half], from_left), right[:, half:]], axis=1)
        self.left = jnp.concatenate([left[:, :half], added(left[:, half:], from_right)], axis=1)
        return self.right, self.left

    def total(self, earlier=None):
        right, left = after((self.right, self.left), earlier)
        got_left = moved(right, self.small, 1)
        got_right = moved(left, self.small, -1)
        return self.piece(0).astype(F32) + got_left.astype(F32) + got_right.astype(F32)


def added(left, right):
    return (left.astype(F32) + right.astype(F32)).astype(BF)


def after(value, earlier):
    return value if earlier is None else lax.optimization_barrier((value, earlier))[0]


def picked(first, value_zero, value_one):
    return jnp.where(first, value_zero, value_one)


def norm_parts(values):
    centered = values - jnp.mean(values, axis=-1, keepdims=True)
    spread = jnp.mean(centered * centered, axis=-1, keepdims=True)
    scale = lax.rsqrt(spread + EPSILON)
    return centered * scale, scale


def layer_norm(values, gain, bias):
    return norm_parts(values)[0] * gain + bias


def layer_norm_back(values, gain, grad):
    unit, scale = norm_parts(values)
    inner = grad * gain
    mean_inner = jnp.mean(inner, axis=-1, keepdims=True)
    mean_cross = jnp.mean(inner * unit, axis=-1, keepdims=True)
    grad_in = scale * (inner - mean_inner - unit * mean_cross)
    return grad_in, unit


NT = (((1,), (1,)), ((), ()))
NN = (((1,), (0,)), ((), ()))


def mxu(left, right, dims=NN):
    return lax.dot_general(left, right, dims, preferred_element_type=F32)


def half_mask(shape, half, axis):
    places = lax.broadcasted_iota(jnp.int32, shape, axis)
    return (places < HEAD_DIM) if half == 0 else (places >= HEAD_DIM)


def whole():
    return pl.BlockSpec(memory_space=pltpu.VMEM)


def called(kernel, name, out_shape, operands, flops, transcendentals):
    shapes = [(o.shape, o.dtype) for o in (*operands, *out_shape)]
    return pl.pallas_call(
        kernel,
        out_shape=out_shape,
        in_specs=[whole()] * len(operands),
        out_specs=[whole()] * len(out_shape),
        compiler_params=pltpu.CompilerParams(vmem_limit_bytes=VMEM_LIMIT),
        cost_estimate=pl.CostEstimate(
            flops=flops,
            bytes_accessed=sum(math.prod(shape) * dtype.itemsize for shape, dtype in shapes),
            transcendentals=transcendentals,
        ),
        name=name,
    )(*operands)


def by_head(block):
    zero = jnp.zeros_like(block)
    return jnp.concatenate([jnp.where(half_mask(block.shape, h, 1), block, zero) for h in range(2)])


def of_heads(rows):
    half = rows.shape[0] // 2
    return jnp.where(half_mask((half, rows.shape[1]), 0, 1), rows[:half], rows[half:])


def attend_kernel(save, q_ref, kv_ref, mark_q_ref, mark_k_ref, out_ref, *kept):
    scaling = jnp.asarray(HEAD_DIM ** (-0.5), BF)
    mark_k = mark_k_ref[...]
    mark_q = jnp.concatenate([mark_q_ref[...]] * 2)
    queries = q_ref.shape[0]
    for pair in range(q_ref.shape[1] // 128):
        q = by_head(q_ref[:, 128 * pair : 128 * pair + 128] * scaling)
        k = kv_ref[:, 256 * pair : 256 * pair + 128]
        v = kv_ref[:, 256 * pair + 128 : 256 * pair + 256]
        q_marked = jnp.concatenate([q, mark_q], axis=1)
        k_marked = jnp.concatenate([k, mark_k], axis=1)
        scores = mxu(q_marked, k_marked, NT)
        top = jnp.max(scores, axis=1, keepdims=True)
        probs = jnp.exp(scores - top).astype(BF)
        out = mxu(probs, jnp.concatenate([v, jnp.ones_like(v)], axis=1))
        total = out[:, 128:]
        out_ref[:, 128 * pair : 128 * pair + 128] = of_heads(out[:, :128] / total).astype(BF)
        if save:
            lse = top + jnp.log(total[:, :1])
            kept[0][:, 2 * pair : 2 * pair + 1] = lse[:queries]
            kept[0][:, 2 * pair + 1 : 2 * pair + 2] = lse[queries:]


def attend(q, kv, mark_q, mark_k, save):
    queries, width = q.shape
    keys = kv.shape[0]
    out_shape = [jax.ShapeDtypeStruct((queries, width), BF)]
    if save:
        out_shape.append(jax.ShapeDtypeStruct((queries, width // HEAD_DIM), F32))
    flops, exps = 16 * queries * keys * width, 2 * queries * keys * width // 128
    return called(
        functools.partial(attend_kernel, save), "attend", out_shape, (q, kv, mark_q, mark_k), flops, exps
    )


def attend_back_kernel(q_ref, kv_ref, do_ref, out_ref, lse_ref, mark_q_ref, mark_k_ref, dq_ref, dkv_ref):
    scaling = jnp.asarray(HEAD_DIM ** (-0.5), BF)
    mark_k = mark_k_ref[...]
    mark_q = jnp.concatenate([mark_q_ref[...]] * 2)
    for pair in range(q_ref.shape[1] // 128):
        columns = slice(128 * pair, 128 * pair + 128)
        q = by_head(q_ref[:, columns] * scaling)
        do = by_head(do_ref[:, columns])
        out = by_head(out_ref[:, columns])
        k = kv_ref[:, 256 * pair : 256 * pair + 128]
        v = kv_ref[:, 256 * pair + 128 : 256 * pair + 256]
        lse = jnp.concatenate([lse_ref[:, 2 * pair : 2 * pair + 1], lse_ref[:, 2 * pair + 1 : 2 * pair + 2]])
        delta = jnp.sum(do.astype(F32) * out.astype(F32), axis=1, keepdims=True)
        q_marked = jnp.concatenate([q, mark_q], axis=1)
        k_marked = jnp.concatenate([k, mark_k], axis=1)
        probs = jnp.exp(mxu(q_marked, k_marked, NT) - lse)
        grad_scores = (probs * (mxu(do, v, NT) - delta)).astype(BF)
        dq_ref[:, columns] = (of_heads(mxu(grad_scores, k)) * HEAD_DIM ** (-0.5)).astype(BF)
        dkv_ref[:, 256 * pair : 256 * pair + 128] = mxu(q.T, grad_scores).T.astype(BF)
        dkv_ref[:, 256 * pair + 128 : 256 * pair + 256] = mxu(do.T, probs.astype(BF)).T.astype(BF)


def project_back_kernel(dq_ref, dkv_ref, w_q_ref, w_kv_ref, own_ref, away_ref):
    rows = dq_ref.shape[0] // 2
    half = dkv_ref.shape[0] // 2
    for at in range(0, own_ref.shape[1], BLOCK):
        columns = slice(at, at + BLOCK)
        by_kv = mxu(dkv_ref[...], w_kv_ref[columns, :], NT)
        by_q = mxu(dq_ref[...], w_q_ref[columns, :], NT)
        own_ref[:rows, columns] = by_kv[:rows] + by_q[:rows]
        own_ref[rows:, columns] = by_kv[rows:half]
        away_ref[:rows, columns] = (by_kv[half : half + rows] + by_q[rows:]).astype(BF)
        away_ref[rows:, columns] = by_kv[half + rows :].astype(BF)


def project_back(dq, dkv, w_q, w_kv):
    keys, width = dkv.shape
    out_shape = [jax.ShapeDtypeStruct((keys // 2, width), kind) for kind in (F32, BF)]
    flops = 2 * keys * width * width
    return called(project_back_kernel, "project_back", out_shape, (dq, dkv, w_q, w_kv), flops, 0)


def attend_back(q, kv, do, out, lse, mark_q, mark_k):
    queries, width = q.shape
    keys = kv.shape[0]
    out_shape = [jax.ShapeDtypeStruct(q.shape, BF), jax.ShapeDtypeStruct(kv.shape, BF)]
    flops, exps = 40 * queries * keys * width, 2 * queries * keys * width // 128
    operands = (q, kv, do, out, lse, mark_q, mark_k)
    return called(attend_back_kernel, "attend_back", out_shape, operands, flops, exps)


def gelu_and_slope(values):
    phi = 0.5 * (1.0 + lax.erf(values * 0.7071067811865476))
    slope = phi + values * (0.3989422804014327 * jnp.exp(-0.5 * values * values))
    return values * phi, slope


def feed_kernel(save, x_ref, joint, out_ref, act_ref, *kept):
    x = x_ref[...]
    width = out_ref.shape[1]
    for at in range(0, 2 * width, BLOCK):
        columns = slice(at, at + BLOCK)
        act, slope = gelu_and_slope(mxu(x, joint[:, columns]))
        act_ref[:, columns] = act.astype(BF)
        if save:
            kept[0][:, columns] = slope.astype(BF)
    for at in range(0, width, BLOCK):
        first, second = 2 * width + at, 3 * width + at
        out_ref[:, at : at + BLOCK] = mxu(act_ref[:, :width], joint[:, first : first + BLOCK]) + mxu(
            act_ref[:, width:], joint[:, second : second + BLOCK]
        )


def feed(x, joint, save):
    rows, width = x.shape
    units = 2 * width
    kept = jax.ShapeDtypeStruct((rows, units), BF)
    out_shape = [jax.ShapeDtypeStruct((rows, width), F32), kept] + ([kept] if save else [])
    flops, exps = 4 * rows * width * units, 2 * rows * units
    return called(functools.partial(feed_kernel, save), "feed", out_shape, (x, joint), flops, exps)


def feed_back_kernel(g_ref, slope_ref, joint, out_ref, grad_ref):
    g = g_ref[...]
    width = out_ref.shape[1]
    for half in range(2):
        for at in range(0, width, BLOCK):
            down = joint[at : at + BLOCK, (2 + half) * width : (3 + half) * width]
            units = slice(half * width + at, half * width + at + BLOCK)
            grad = mxu(g, down, NT) * slope_ref[:, units].astype(F32)
            grad_ref[:, units] = grad.astype(BF)
    for at in range(0, width, BLOCK):
        rows = slice(at, at + BLOCK)
        out_ref[:, rows] = mxu(grad_ref[...], joint[rows, : 2 * width], NT)


def feed_back(g, slope, joint):
    rows, width = g.shape
    units = 2 * width
    out_shape = [jax.ShapeDtypeStruct((rows, width), F32), jax.ShapeDtypeStruct((rows, units), BF)]
    return called(feed_back_kernel, "feed_back", out_shape, (g, slope, joint), 4 * rows * width * units, 0)


def dot(left, right, dims=NN):
    return lax.dot_general(left, right, dims, preferred_element_type=F32)


def from_other(part):
    half = part.shape[0] // 2
    other = swapped(part.astype(BF)).astype(F32)
    return jnp.concatenate([other[half:], other[:half]])


class Forward:
    def __init__(self, start, ring, marks, norms, received=None):
        self.ring, self.marks, self.norms = ring, marks, norms
        self.start, self.received = start, received
        self.rows = start.shape[0]

    def norm(self, earlier=None):
        hidden_low = self.start
        if self.received is not None:
            received = after(self.received, earlier)
            hidden_low = jnp.where(lax.axis_index("section") == 0, self.start, received)
        self.hidden = hidden_low.astype(F32)
        self.hidden_other = swapped(hidden_low)
        normed = layer_norm(self.hidden, self.norms[0], self.norms[1]).astype(BF)
        self.normed = normed
        self.near = fetched(normed, self.ring, 1), fetched(normed, self.ring, 3)

    def fetch_raw(self, earlier):
        self.hidden_low = after(self.start, earlier)
        self.hidden_other = swapped(self.hidden_low)
        self.near = fetched(self.hidden_low, self.ring, 1), fetched(self.hidden_low, self.ring, 3)
        self.fetch_far()

    def collect_raw(self):
        self.hidden = self.hidden_low.astype(F32)
        plus, minus = self.near
        ring_rows = jnp.concatenate([self.hidden_low, plus, *self.far, minus])
        rows = jnp.concatenate([ring_rows, swapped(ring_rows)]).astype(F32)
        self.normed_all = layer_norm(rows, self.norms[0], self.norms[1]).astype(BF)
        half = 4 * self.rows
        self.normed_chip = jnp.concatenate(
            [self.normed_all[: self.rows], self.normed_all[half : half + self.rows]]
        )

    def swap_near(self):
        plus, minus = self.near
        self.other_near = swapped(jnp.concatenate([self.normed, plus, minus]))

    def fetch_far(self):
        plus, minus = self.near
        half = self.rows // 2
        self.far = fetched(plus[:half], self.ring, 1), fetched(minus[half:], self.ring, 3)

    def collect(self, earlier=None):
        rows, normed = self.rows, self.normed
        plus, minus = self.near
        two = jnp.concatenate(after(self.far, earlier))
        other_near, other_two = self.other_near, swapped(two)
        self.normed_all = jnp.concatenate(
            [normed, plus, two, minus, other_near[: 2 * rows], other_two, other_near[2 * rows :]]
        )
        self.normed_chip = jnp.concatenate([normed, other_near[:rows]])

    def project(self, weights, earlier):
        normed_all, normed_chip = after((self.normed_all, self.normed_chip), earlier)
        self.kv = dot(normed_all, weights["kv"]).astype(BF)
        self.q = dot(normed_chip, weights["q"]).astype(BF)

    def attention(self, save):
        self.attended, *self.lse = attend(self.q, self.kv, *self.marks, save)

    def feed_forward(self, weights, save, arrivals, between):
        rows = self.rows
        part = dot(self.attended, weights["out"])
        hidden = jnp.concatenate([self.hidden, self.hidden_other.astype(F32)])
        self.middle = hidden + part + from_other(part)
        normed_ffn = layer_norm(self.middle, self.norms[2], self.norms[3]).astype(BF)
        self.normed_ffn = after(normed_ffn, arrivals)
        fed, self.act, *self.slope = feed(self.normed_ffn, weights["feed"], save)
        self.fed = fed = after(fed, between)
        self.result = (self.middle[:rows] + fed[:rows] + swapped(fed[rows:].astype(BF)).astype(F32)).astype(BF)


class Backward:
    def __init__(self, grad_low, forward):
        self.grad_low, self.forward = grad_low, forward
        self.rows = grad_low.shape[0]
        self.grad_chip = jnp.concatenate([grad_low, swapped(grad_low)])

    def feed_forward(self, weights, earlier, arrivals):
        rows, forward = self.rows, self.forward
        grad_chip = after(self.grad_chip, earlier)
        back, self.grad_up = feed_back(grad_chip, *forward.slope, weights["feed"])
        back = after(back, arrivals)
        grad_normed = back + from_other(back)
        gain = forward.norms[2]
        part, unit = layer_norm_back(forward.middle, gain, grad_normed)
        self.grad_gain_ffn = jnp.sum(grad_normed[:rows] * unit[:rows], axis=0)
        self.grad_bias_ffn = jnp.sum(grad_normed[:rows], axis=0)
        grad_middle = grad_chip.astype(F32) + part
        self.grad_middle = grad_middle[:rows]
        self.grad_middle_low = grad_middle.astype(BF)
        self.grad_heads = dot(self.grad_middle_low, weights["out"], NT).astype(BF)

    def attention(self, earlier):
        forward = self.forward
        grad_heads = after(self.grad_heads, earlier)
        self.dq, self.dkv = attend_back(
            forward.q, forward.kv, grad_heads, forward.attended, *forward.lse, *forward.marks
        )

    def project(self, weights, earlier=None):
        dq, dkv = after((self.dq, self.dkv), earlier)
        self.own, self.away = project_back(dq, dkv, weights["q"], weights["kv"])

    def sum_cores(self, earlier=None):
        rows = self.rows
        own, away = after((self.own, self.away), earlier)
        far = swapped(away[2 * rows : 3 * rows])
        near = swapped(jnp.concatenate([away[: 2 * rows], away[3 * rows :]]))
        self.ring_grads = [
            own[d * rows : (d + 1) * rows] + part.astype(F32)
            for d, part in enumerate((near[:rows], near[rows : 2 * rows], far, near[2 * rows :]))
        ]

    def piece(self, steps, lower=0, upper=None):
        return self.ring_grads[steps][lower : self.rows if upper is None else upper]

    def spread_far(self):
        half, ring = self.rows // 2, self.forward.ring
        self.far = (
            moved(self.piece(2, 0, half).astype(BF), ring, 1),
            moved(self.piece(2, half).astype(BF), ring, -1),
        )

    def spread_near(self, earlier=None):
        half, ring = self.rows // 2, self.forward.ring
        from_left, from_right = after(self.far, earlier)
        right = jnp.concatenate([self.piece(1, 0, half) + from_left.astype(F32), self.piece(1, half)])
        left = jnp.concatenate([self.piece(3, 0, half), self.piece(3, half) + from_right.astype(F32)])
        self.near = moved(right.astype(BF), ring, 1), moved(left.astype(BF), ring, -1)

    def reduce(self, earlier=None):
        forward = self.forward
        grad_normed = self.piece(0)
        for part in after(self.near, earlier):
            grad_normed = grad_normed + part.astype(F32)
        part, unit = layer_norm_back(forward.hidden, forward.norms[0], grad_normed)
        self.grad_gain_attn = jnp.sum(grad_normed * unit, axis=0)
        self.grad_bias_attn = jnp.sum(grad_normed, axis=0)
        self.grad_hidden_low = (self.grad_middle + part).astype(BF)

    def vectors(self):
        return jnp.stack([self.grad_gain_attn, self.grad_bias_attn, self.grad_gain_ffn, self.grad_bias_ffn])


def marks_of(lengths, place, rows, core):
    index = lax.iota(jnp.int32, 8 * rows)
    core_at = jnp.where(index < 4 * rows, core, 1 - core)
    chip_at = lax.rem(place + lax.rem(index // rows, 4), 4)
    positions = chip_at * (2 * rows) + core_at * rows + lax.rem(index, rows)
    cells = lengths.shape[0]
    bounds = jnp.cumsum(lengths)
    segments = jnp.sum((positions[:, None] >= bounds[None, :]).astype(jnp.int32), axis=1, keepdims=True)
    places = lax.broadcasted_iota(jnp.int32, (1, 128), 1)
    own = segments == places
    mark_q = jnp.where(own | (places >= cells), 0.0, MASKED).astype(BF)
    mark_k = own.astype(BF)
    return jnp.concatenate([mark_q[:rows], mark_q[4 * rows : 5 * rows]]), mark_k


def arrange_kernel(qkv_ref, out_ref, vectors_ref, mine_ref, other_ref):
    width = out_ref.shape[1]
    half = width // 2
    core = lax.axis_index("core")
    for at_core, target in ((core, mine_ref), (1 - core, other_ref)):
        start = at_core * half

        def columns(base, size):
            return pl.ds(pl.multiple_of(start + base, 128), size)

        for pair in range(half // 128):
            target[:, 256 * pair : 256 * pair + 128] = qkv_ref[:, columns(width + 128 * pair, 128)]
            target[:, 256 * pair + 128 : 256 * pair + 256] = qkv_ref[:, columns(2 * width + 128 * pair, 128)]
        target[:, width : width + half] = qkv_ref[:, columns(0, half)]
        target[:, width + half : 2 * width] = out_ref[:, columns(0, half)]
        target[:, 2 * width :] = vectors_ref[...]


def attention_shards(w_qkv, w_out, vectors, core_zero):
    rows, width = w_out.shape
    columns = jnp.pad(vectors.T, ((0, 0), (0, 128 - vectors.shape[0])))
    out_shape = [jax.ShapeDtypeStruct((rows, 2 * width + 128), BF)] * 2
    mine, other = called(arrange_kernel, "arrange", out_shape, (w_qkv, w_out, columns), 0, 0)
    other = swapped(other)
    both = jnp.concatenate([picked(core_zero, mine, other), picked(core_zero, other, mine)])
    return both[:, :width], both[:, width:]


def exchanged_in(zero, one, core_zero):
    mine = picked(core_zero, zero, one)
    other = swapped(picked(core_zero, one, zero))
    return jnp.concatenate([picked(core_zero, mine, other), picked(core_zero, other, mine)])


def feed_shard(w_up, w_down, core_zero):
    rows = w_up.shape[0]
    units = w_up.reshape(rows, 16, 2, 2, -1).transpose(2, 0, 3, 1, 4).reshape(2, rows, -1)
    up = exchanged_in(units[0], units[1], core_zero)
    half = w_down.shape[0] // 2
    return jnp.concatenate([up, w_down[:half], w_down[half:]], axis=1)


def out_rows(out_half, core_zero):
    half = out_half.shape[1]
    zero, one = out_half[:half], out_half[half:]
    mine = picked(core_zero, zero, one)
    other = swapped(picked(core_zero, one, zero))
    return jnp.concatenate([picked(core_zero, mine, other), picked(core_zero, other, mine)], axis=1)


TN = (((0,), (0,)), ((), ()))


def summed(lefts, rights):
    return dot(jnp.concatenate(lefts), jnp.concatenate(rights), TN)


def feed_grads(backs):
    forwards = [back.forward for back in backs]
    width = backs[0].grad_chip.shape[1]
    up = summed([f.normed_ffn for f in forwards], [back.grad_up for back in backs])
    act = jnp.concatenate([f.act for f in forwards])
    grads = jnp.concatenate([back.grad_chip for back in backs])
    down = [dot(act[:, h * width : (h + 1) * width], grads, TN) for h in range(2)]
    return jnp.concatenate([up.astype(BF)] + [part.astype(BF) for part in down], axis=1)


def out_grads(backs, core_zero):
    grads = summed([back.forward.attended for back in backs], [back.grad_middle_low for back in backs])
    grads = grads.astype(BF)
    half = grads.shape[0]
    zero, one = grads[:, :half], grads[:, half:]
    mine = picked(core_zero, zero, one)
    other = swapped(picked(core_zero, one, zero))
    return jnp.concatenate([picked(core_zero, mine, other), picked(core_zero, other, mine)])


def query_grads(backs):
    return summed([back.forward.normed_chip for back in backs], [back.dq for back in backs]).astype(BF)


def key_value_grads(backs, earlier):
    dkv = after([back.dkv for back in backs], earlier)
    return summed([back.forward.normed_all for back in backs], dkv).astype(BF)


def vector_grads(backs):
    vectors = sum(back.vectors() for back in backs)
    vectors = jnp.pad(vectors, ((0, 128 - vectors.shape[0]), (0, 0))).astype(BF)
    return added(vectors, swapped(vectors)).T


def exchanged_out(shard, core_zero):
    rows = shard.shape[0] // 2
    zero, one = shard[:rows], shard[rows:]
    mine = picked(core_zero, zero, one)
    other = swapped(picked(core_zero, one, zero).astype(BF)).astype(F32)
    return picked(core_zero, mine, other), picked(core_zero, other, mine)


SOURCES = ((1, 2), (2, 1), (3, 0))


def whole_features(inputs, cotangents, section):
    turned = transposed(jnp.stack([inputs[1], cotangents[1]]))
    inputs = jnp.stack([inputs[0], turned[0]])
    cotangents = jnp.stack([cotangents[0], turned[1]])
    one, two, three = (
        lax.ppermute(picked(section == a, inputs, cotangents), "section", [(a, 0), (b, 3)]) for a, b in SOURCES
    )
    start = jnp.concatenate([inputs, one, two, three], axis=2)
    last = jnp.concatenate([three, two, one, cotangents], axis=2)
    return start, last


def spread_features(grads, outputs, section):
    width = grads.shape[2] // 4

    def piece(value, z):
        return value[:, :, z * width : (z + 1) * width]

    one, two, three = (
        lax.ppermute(picked(section == 0, piece(grads, a), piece(outputs, b)), "section", [(0, a), (3, b)])
        for a, b in SOURCES
    )

    def by_section(values):
        result = values[3]
        for z in range(3):
            result = jnp.where(section == z, values[z], result)
        return result

    grads = by_section((piece(grads, 0), one, two, three))
    outputs = by_section((three, two, one, piece(outputs, 3)))
    turned = transposed(jnp.stack([grads[1], outputs[1]]))
    return jnp.stack([grads[0], turned[0]]), jnp.stack([outputs[0], turned[1]])


def local(
    block_input,
    cotangent,
    cell_lengths,
    norm_attn_gain,
    norm_attn_bias,
    w_qkv,
    w_out,
    norm_ffn_gain,
    norm_ffn_bias,
    w_up,
    w_down,
):
    section = lax.axis_index("section")
    at_x = lax.axis_index("dp")
    at_y = lax.axis_index("y")
    core = lax.axis_index("core")
    core_zero = core == 0
    sections = lax.axis_size("section")
    rows = block_input.shape[1]
    rings = ("y", "dp")
    width = w_out.shape[2]
    half = width // 2

    feed_whole = lax.all_gather(feed_shard(w_up[0], w_down[0], core_zero), ("dp", "y"), axis=0, tiled=True)
    vectors = jnp.concatenate([norm_attn_gain, norm_attn_bias, norm_ffn_gain, norm_ffn_bias])
    kv_shard, rest_shard = attention_shards(w_qkv[0], w_out[0], vectors, core_zero)
    kv, rest = Gather([kv_shard], "dp", "y"), Gather([rest_shard], "y", "dp")
    start, last_grad = whole_features(block_input, cotangent, section)
    passes = [Forward(start[m], rings[m], None, None) for m in range(2)]
    kv.neighbours((start, last_grad))
    rest.neighbours((start, last_grad))
    kv.along_first()
    rest.along_first()
    near = kv.along_second() + rest.along_second()
    for now in passes:
        now.fetch_raw(near)
    marks = (
        marks_of(cell_lengths[2 * at_x], at_y, rows, core),
        marks_of(cell_lengths[2 * at_y + 1], at_x, rows, core),
    )
    (w_kv,) = kv.placed()
    (rest_whole,) = rest.placed()
    weights = {"kv": w_kv, "q": rest_whole[:, :half], "out": out_rows(rest_whole[:, half:width], core_zero)}
    norms = rest_whole[:, width:].T[:4].astype(F32)
    norms = tuple(norms[i : i + 1] for i in range(4))
    for m, now in enumerate(passes):
        now.marks, now.norms = marks[m], norms
        now.collect_raw()
    weights["feed"] = feed_whole

    forward_pairs = [(s, s + 1) for s in range(sections - 1)]
    result = None
    for step in range(sections):
        final = step == sections - 1
        for m in range(2):
            now, other = passes[m], passes[1 - m]
            waiting = step + m > 0 and not (final and m == 1)
            now.project(weights, result)
            now.attention(final)
            if waiting:
                other.norm(now.attended)
                now.attended = after(now.attended, other.normed)
                other.swap_near()
                other.fetch_far()
            now.feed_forward(
                weights, final, other.near if waiting else None, other.other_near if waiting else None
            )
            if waiting:
                other.collect(now.fed)
            result = now.result
            if not final:
                received = lax.ppermute(result, "section", forward_pairs)
                passes[m] = Forward(start[m], rings[m], marks[m], norms, received)
    block_output = jnp.stack([now.result for now in passes])

    backs = [Backward(last_grad[m], passes[m]) for m in range(2)]
    backward_pairs = [(s + 1, s) for s in range(sections - 1)]
    earlier = result
    for step in range(sections):
        final = step == sections - 1
        for m in range(2):
            now, other = backs[m], backs[1 - m]
            waiting = step + m > 0
            now.feed_forward(weights, earlier, other.far if waiting else None)
            if waiting:
                other.spread_near()
            if final and m == 1:
                break
            now.attention(None)
            if waiting:
                other.reduce(now.dkv)
                now.project(weights, other.grad_hidden_low)
                received = lax.ppermute(other.grad_hidden_low, "section", backward_pairs)
                received = after(received, now.own)
                grad_low = jnp.where(section == sections - 1, last_grad[1 - m], received)
                backs[1 - m] = Backward(grad_low, passes[1 - m])
                now.sum_cores(grad_low)
            else:
                now.project(weights)
                now.sum_cores()
            now.spread_far()
            earlier = now.ring_grads

    joint = feed_grads(backs)
    backs[0].reduce()
    backs[1].attention((backs[0].grad_hidden_low, joint))
    joint = lax.psum_scatter(joint, ("dp", "y"), scatter_dimension=0, tiled=True).astype(F32)
    backs[1].project(weights)
    backs[1].sum_cores()
    backs[1].spread_far()
    backs[1].spread_near()
    kv_part = key_value_grads(backs, backs[1].far)
    out_part = out_grads(backs, core_zero)
    query_part = query_grads(backs)
    backs[1].reduce((kv_part, query_part))
    sum_kv = Scatter([after(kv_part, backs[1].near)], "y", "dp")
    sum_rest = Scatter([query_part, out_part, vector_grads(backs)], "dp", "y")
    sum_kv.far()
    sum_rest.far()
    sum_kv.near()
    sum_rest.near()
    mine = sum_kv.bundle(), sum_rest.bundle()
    sum_kv.mine, sum_rest.mine = after(mine, mine[::-1])
    small = sum_kv.small_far() + sum_rest.small_far()
    own_rows = w_out.shape[1]
    up_grads = joint[:, : 2 * width]
    grad_down = jnp.concatenate([joint[:, 2 * width : 3 * width], joint[:, 3 * width :]])
    units = jnp.stack(exchanged_out(up_grads, core_zero), axis=1)
    units = units.reshape(own_rows, 2, 2, 16, -1).transpose(0, 3, 1, 2, 4)
    grad_up = units.reshape(own_rows, -1)
    input_grad = after(jnp.stack([now.grad_hidden_low for now in backs]), small)
    input_grad, block_output = spread_features(input_grad, block_output, section)
    kv_grads = after(sum_kv.total(), grad_up)
    rest_grads = sum_rest.total()

    kv_cores = exchanged_out(kv_grads, core_zero)
    rest_cores = exchanged_out(rest_grads[:, :width], core_zero)
    keys, values = [], []
    for part in kv_cores:
        for pair in range(half // 128):
            keys.append(part[:, 256 * pair : 256 * pair + 128])
            values.append(part[:, 256 * pair + 128 : 256 * pair + 256])
    grad_qkv = jnp.concatenate([rest_cores[0][:, :half], rest_cores[1][:, :half]] + keys + values, axis=1)
    grad_out = jnp.concatenate([rest_cores[0][:, half:width], rest_cores[1][:, half:width]], axis=1)
    columns = rest_grads[:, width:]
    grad_vectors = picked(core_zero, columns[:own_rows], columns[own_rows:]).T[:4]
    return (
        block_output,
        input_grad.astype(F32),
        grad_vectors[0:1],
        grad_vectors[1:2],
        grad_qkv[None],
        grad_out[None],
        grad_vectors[2:3],
        grad_vectors[3:4],
        grad_up[None],
        grad_down[None],
    )


def solution(mesh):
    sizes = mesh.devices.shape
    cores = Mesh(mesh.devices.reshape(sizes[0], sizes[1], sizes[2] // 2, 2), ("section", "dp", "y", "core"))
    seq = ("y", "core")
    plane = ("dp", "y", "core")
    rows = P("dp", seq, "section")
    vector = P("section", plane)
    matrix = P("section", plane, None)
    return jax.shard_map(
        local,
        mesh=cores,
        in_specs=(rows, rows, P(), vector, vector, matrix, matrix, vector, vector, matrix, matrix),
        out_specs=(rows, rows, vector, vector, matrix, matrix, vector, vector, matrix, matrix),
        check_vma=False,
    )
```

```python
import functools
import math

import jax
import jax.numpy as jnp
from jax import lax
from jax.experimental import pallas as pl
from jax.experimental.pallas import tpu as pltpu
from jax.sharding import Mesh, PartitionSpec as P

HEAD_DIM = 64
EPSILON = 1e-05
MASKED = -1e30
BF = jnp.bfloat16
F32 = jnp.float32
BLOCK = 256
VMEM_LIMIT = 20 * 1024 * 1024


def moved(value, axis, steps):
    count = lax.axis_size(axis)
    return lax.ppermute(value, axis, [(i, (i + steps) % count) for i in range(count)])


def fetched(value, axis, steps):
    return moved(value, axis, -steps)


def swapped(value):
    return moved(value, "core", 1)


def transposed(value):
    rows, columns = lax.axis_size("dp"), lax.axis_size("y")
    pairs = [(x * columns + y, y * columns + x) for x in range(rows) for y in range(columns)]
    return lax.ppermute(value, ("dp", "y"), pairs)


def place_kernel(first, second, group, *refs):
    own, plus, two_a, two_b, minus = refs[:5]
    outs = refs[5 : 5 + group]
    sems = refs[5 + group]
    count = 4
    f = lax.axis_index(first)
    s = lax.axis_index(second)
    copies = []
    for e in range(count):
        for d in range(count):
            if e == 0:
                source = own.at[d]
            elif e == 1:
                source = plus.at[d]
            elif e == 3:
                source = minus.at[d]
            elif d < 2:
                source = two_a.at[d]
            else:
                source = two_b.at[d - 2]
            f_at = lax.rem(f + d, count)
            s_at = lax.rem(s + e, count)
            chip = f_at * count + s_at if first == "dp" else s_at * count + f_at
            for g in range(group):
                copies.append(
                    pltpu.make_async_copy(source.at[g], outs[g].at[chip], sems.at[len(copies)])
                )
    for copy in copies:
        copy.start()
    for copy in copies:
        copy.wait()


def split_at(columns):
    return columns // 256 * 128


class Gather:
    def __init__(self, shards, first, second):
        self.first, self.second, self.group = first, second, len(shards)
        self.shard = jnp.stack(shards)

    def neighbours(self, earlier=None):
        shard = after(self.shard, earlier)
        self.near = fetched(shard, self.first, 1), fetched(shard, self.first, 3)
        return self.near

    def along_first(self):
        plus, minus = self.near
        half = split_at(plus.shape[-1])
        two_a = fetched(plus[..., :half], self.first, 1)
        two_b = fetched(minus[..., half:], self.first, 3)
        two = jnp.concatenate([two_a, two_b], axis=-1)
        self.bundle = jnp.stack([self.shard, plus, two, minus])
        return self.bundle

    def along_second(self, earlier=None):
        bundle = after(self.bundle, earlier)
        self.plus = fetched(bundle, self.second, 1)
        self.minus = fetched(bundle, self.second, 3)
        return self.plus, self.minus

    def placed(self):
        two_a = fetched(self.plus[:2], self.second, 1)
        two_b = fetched(self.minus[2:], self.second, 3)
        rows, columns = self.shard.shape[1:]
        wholes = pl.pallas_call(
            functools.partial(place_kernel, self.first, self.second, self.group),
            out_shape=[jax.ShapeDtypeStruct((16, rows, columns), self.shard.dtype)] * self.group,
            in_specs=[pl.BlockSpec(memory_space=pltpu.VMEM)] * 5,
            out_specs=[pl.BlockSpec(memory_space=pl.ANY)] * self.group,
            scratch_shapes=[pltpu.SemaphoreType.DMA((16 * self.group,))],
            compiler_params=pltpu.CompilerParams(vmem_limit_bytes=VMEM_LIMIT),
            name="place_" + self.first,
        )(self.bundle, self.plus, two_a, two_b, self.minus)
        return [whole.reshape(16 * rows, columns) for whole in wholes]


class Scatter:
    def __init__(self, wholes, big, small):
        self.big, self.small = big, small
        self.grids = [whole.reshape((4, 4, whole.shape[0] // 16, whole.shape[1])) for whole in wholes]
        self.along = 0 if big == "dp" else 1
        self.at_big = lax.axis_index(big)
        self.at_small = lax.axis_index(small)

    def chunk(self, steps, lower=0, upper=4):
        at = lax.rem(self.at_big + steps, 4)
        parts = []
        for grid in self.grids:
            part = lax.dynamic_index_in_dim(grid, at, self.along, keepdims=False)
            parts.append(part[lower:upper])
        return parts[0] if len(parts) == 1 else jnp.concatenate(parts, axis=-1)

    def far(self):
        self.far_right, self.far_left = self.chunk(2, 0, 2), self.chunk(2, 2, 4)
        return self.far_right, self.far_left

    def near(self, earlier=None):
        far_right, far_left = after((self.far_right, self.far_left), earlier)
        from_left = moved(far_right, self.big, 1)
        from_right = moved(far_left, self.big, -1)
        self.right = jnp.concatenate([added(self.chunk(1, 0, 2), from_left), self.chunk(1, 2, 4)])
        self.left = jnp.concatenate([self.chunk(3, 0, 2), added(self.chunk(3, 2, 4), from_right)])
        return self.right, self.left

    def bundle(self, earlier=None):
        right, left = after((self.right, self.left), earlier)
        got_left = moved(right, self.big, 1)
        got_right = moved(left, self.big, -1)
        mine = self.chunk(0).astype(F32) + got_left.astype(F32) + got_right.astype(F32)
        self.mine = mine.astype(BF)
        return self.mine

    def piece(self, steps):
        return lax.dynamic_index_in_dim(self.mine, lax.rem(self.at_small + steps, 4), 0, keepdims=False)

    def small_far(self):
        far = self.piece(2)
        half = split_at(far.shape[-1])
        from_left = moved(far[:, :half], self.small, 1)
        from_right = moved(far[:, half:], self.small, -1)
        right, left = self.piece(1), self.piece(3)
        self.right = jnp.concatenate([added(right[:, :half], from_left), right[:, half:]], axis=1)
        self.left = jnp.concatenate([left[:, :half], added(left[:, half:], from_right)], axis=1)
        return self.right, self.left

    def total(self, earlier=None):
        right, left = after((self.right, self.left), earlier)
        got_left = moved(right, self.small, 1)
        got_right = moved(left, self.small, -1)
        return self.piece(0).astype(F32) + got_left.astype(F32) + got_right.astype(F32)


def added(left, right):
    return (left.astype(F32) + right.astype(F32)).astype(BF)


def after(value, earlier):
    return value if earlier is None else lax.optimization_barrier((value, earlier))[0]


def picked(first, value_zero, value_one):
    return jnp.where(first, value_zero, value_one)


def norm_parts(values):
    centered = values - jnp.mean(values, axis=-1, keepdims=True)
    spread = jnp.mean(centered * centered, axis=-1, keepdims=True)
    scale = lax.rsqrt(spread + EPSILON)
    return centered * scale, scale


def layer_norm(values, gain, bias):
    return norm_parts(values)[0] * gain + bias


def layer_norm_back(values, gain, grad):
    unit, scale = norm_parts(values)
    inner = grad * gain
    mean_inner = jnp.mean(inner, axis=-1, keepdims=True)
    mean_cross = jnp.mean(inner * unit, axis=-1, keepdims=True)
    grad_in = scale * (inner - mean_inner - unit * mean_cross)
    return grad_in, unit


NT = (((1,), (1,)), ((), ()))
NN = (((1,), (0,)), ((), ()))


def mxu(left, right, dims=NN):
    return lax.dot_general(left, right, dims, preferred_element_type=F32)


def half_mask(shape, half, axis):
    places = lax.broadcasted_iota(jnp.int32, shape, axis)
    return (places < HEAD_DIM) if half == 0 else (places >= HEAD_DIM)


def whole():
    return pl.BlockSpec(memory_space=pltpu.VMEM)


def called(kernel, name, out_shape, operands, flops, transcendentals):
    shapes = [(o.shape, o.dtype) for o in (*operands, *out_shape)]
    return pl.pallas_call(
        kernel,
        out_shape=out_shape,
        in_specs=[whole()] * len(operands),
        out_specs=[whole()] * len(out_shape),
        compiler_params=pltpu.CompilerParams(vmem_limit_bytes=VMEM_LIMIT),
        cost_estimate=pl.CostEstimate(
            flops=flops,
            bytes_accessed=sum(math.prod(shape) * dtype.itemsize for shape, dtype in shapes),
            transcendentals=transcendentals,
        ),
        name=name,
    )(*operands)


def by_head(block):
    zero = jnp.zeros_like(block)
    return jnp.concatenate([jnp.where(half_mask(block.shape, h, 1), block, zero) for h in range(2)])


def of_heads(rows):
    half = rows.shape[0] // 2
    return jnp.where(half_mask((half, rows.shape[1]), 0, 1), rows[:half], rows[half:])


def attend_kernel(save, q_ref, kv_ref, mark_q_ref, mark_k_ref, out_ref, *kept):
    scaling = jnp.asarray(HEAD_DIM ** (-0.5), BF)
    mark_k = mark_k_ref[...]
    mark_q = jnp.concatenate([mark_q_ref[...]] * 2)
    queries = q_ref.shape[0]
    for pair in range(q_ref.shape[1] // 128):
        q = by_head(q_ref[:, 128 * pair : 128 * pair + 128] * scaling)
        k = kv_ref[:, 256 * pair : 256 * pair + 128]
        v = kv_ref[:, 256 * pair + 128 : 256 * pair + 256]
        q_marked = jnp.concatenate([q, mark_q], axis=1)
        k_marked = jnp.concatenate([k, mark_k], axis=1)
        scores = mxu(q_marked, k_marked, NT)
        top = jnp.max(scores, axis=1, keepdims=True)
        probs = jnp.exp(scores - top).astype(BF)
        out = mxu(probs, jnp.concatenate([v, jnp.ones_like(v)], axis=1))
        total = out[:, 128:]
        out_ref[:, 128 * pair : 128 * pair + 128] = of_heads(out[:, :128] / total).astype(BF)
        if save:
            lse = top + jnp.log(total[:, :1])
            kept[0][:, 2 * pair : 2 * pair + 1] = lse[:queries]
            kept[0][:, 2 * pair + 1 : 2 * pair + 2] = lse[queries:]


def attend(q, kv, mark_q, mark_k, save):
    queries, width = q.shape
    keys = kv.shape[0]
    out_shape = [jax.ShapeDtypeStruct((queries, width), BF)]
    if save:
        out_shape.append(jax.ShapeDtypeStruct((queries, width // HEAD_DIM), F32))
    flops, exps = 16 * queries * keys * width, 2 * queries * keys * width // 128
    return called(
        functools.partial(attend_kernel, save), "attend", out_shape, (q, kv, mark_q, mark_k), flops, exps
    )


def attend_back_kernel(q_ref, kv_ref, do_ref, out_ref, lse_ref, mark_q_ref, mark_k_ref, dq_ref, dkv_ref):
    scaling = jnp.asarray(HEAD_DIM ** (-0.5), BF)
    mark_k = mark_k_ref[...]
    mark_q = jnp.concatenate([mark_q_ref[...]] * 2)
    for pair in range(q_ref.shape[1] // 128):
        columns = slice(128 * pair, 128 * pair + 128)
        q = by_head(q_ref[:, columns] * scaling)
        do = by_head(do_ref[:, columns])
        out = by_head(out_ref[:, columns])
        k = kv_ref[:, 256 * pair : 256 * pair + 128]
        v = kv_ref[:, 256 * pair + 128 : 256 * pair + 256]
        lse = jnp.concatenate([lse_ref[:, 2 * pair : 2 * pair + 1], lse_ref[:, 2 * pair + 1 : 2 * pair + 2]])
        delta = jnp.sum(do.astype(F32) * out.astype(F32), axis=1, keepdims=True)
        q_marked = jnp.concatenate([q, mark_q], axis=1)
        k_marked = jnp.concatenate([k, mark_k], axis=1)
        probs = jnp.exp(mxu(q_marked, k_marked, NT) - lse)
        grad_scores = (probs * (mxu(do, v, NT) - delta)).astype(BF)
        dq_ref[:, columns] = (of_heads(mxu(grad_scores, k)) * HEAD_DIM ** (-0.5)).astype(BF)
        dkv_ref[:, 256 * pair : 256 * pair + 128] = mxu(q.T, grad_scores).T.astype(BF)
        dkv_ref[:, 256 * pair + 128 : 256 * pair + 256] = mxu(do.T, probs.astype(BF)).T.astype(BF)


def project_back_kernel(dq_ref, dkv_ref, w_q_ref, w_kv_ref, own_ref, away_ref):
    rows = dq_ref.shape[0] // 2
    half = dkv_ref.shape[0] // 2
    for at in range(0, own_ref.shape[1], BLOCK):
        columns = slice(at, at + BLOCK)
        by_kv = mxu(dkv_ref[...], w_kv_ref[columns, :], NT)
        by_q = mxu(dq_ref[...], w_q_ref[columns, :], NT)
        own_ref[:rows, columns] = by_kv[:rows] + by_q[:rows]
        own_ref[rows:, columns] = by_kv[rows:half]
        away_ref[:rows, columns] = (by_kv[half : half + rows] + by_q[rows:]).astype(BF)
        away_ref[rows:, columns] = by_kv[half + rows :].astype(BF)


def project_back(dq, dkv, w_q, w_kv):
    keys, width = dkv.shape
    out_shape = [jax.ShapeDtypeStruct((keys // 2, width), kind) for kind in (F32, BF)]
    flops = 2 * keys * width * width
    return called(project_back_kernel, "project_back", out_shape, (dq, dkv, w_q, w_kv), flops, 0)


def attend_back(q, kv, do, out, lse, mark_q, mark_k):
    queries, width = q.shape
    keys = kv.shape[0]
    out_shape = [jax.ShapeDtypeStruct(q.shape, BF), jax.ShapeDtypeStruct(kv.shape, BF)]
    flops, exps = 40 * queries * keys * width, 2 * queries * keys * width // 128
    operands = (q, kv, do, out, lse, mark_q, mark_k)
    return called(attend_back_kernel, "attend_back", out_shape, operands, flops, exps)


def gelu_and_slope(values):
    phi = 0.5 * (1.0 + lax.erf(values * 0.7071067811865476))
    slope = phi + values * (0.3989422804014327 * jnp.exp(-0.5 * values * values))
    return values * phi, slope


def feed_kernel(save, x_ref, joint, out_ref, act_ref, *kept):
    x = x_ref[...]
    width = out_ref.shape[1]
    for at in range(0, 2 * width, BLOCK):
        columns = slice(at, at + BLOCK)
        act, slope = gelu_and_slope(mxu(x, joint[:, columns]))
        act_ref[:, columns] = act.astype(BF)
        if save:
            kept[0][:, columns] = slope.astype(BF)
    for at in range(0, width, BLOCK):
        first, second = 2 * width + at, 3 * width + at
        out_ref[:, at : at + BLOCK] = mxu(act_ref[:, :width], joint[:, first : first + BLOCK]) + mxu(
            act_ref[:, width:], joint[:, second : second + BLOCK]
        )


def feed(x, joint, save):
    rows, width = x.shape
    units = 2 * width
    kept = jax.ShapeDtypeStruct((rows, units), BF)
    out_shape = [jax.ShapeDtypeStruct((rows, width), F32), kept] + ([kept] if save else [])
    flops, exps = 4 * rows * width * units, 2 * rows * units
    return called(functools.partial(feed_kernel, save), "feed", out_shape, (x, joint), flops, exps)


def feed_back_kernel(g_ref, slope_ref, joint, out_ref, grad_ref):
    g = g_ref[...]
    width = out_ref.shape[1]
    for half in range(2):
        for at in range(0, width, BLOCK):
            down = joint[at : at + BLOCK, (2 + half) * width : (3 + half) * width]
            units = slice(half * width + at, half * width + at + BLOCK)
            grad = mxu(g, down, NT) * slope_ref[:, units].astype(F32)
            grad_ref[:, units] = grad.astype(BF)
    for at in range(0, width, BLOCK):
        rows = slice(at, at + BLOCK)
        out_ref[:, rows] = mxu(grad_ref[...], joint[rows, : 2 * width], NT)


def feed_back(g, slope, joint):
    rows, width = g.shape
    units = 2 * width
    out_shape = [jax.ShapeDtypeStruct((rows, width), F32), jax.ShapeDtypeStruct((rows, units), BF)]
    return called(feed_back_kernel, "feed_back", out_shape, (g, slope, joint), 4 * rows * width * units, 0)


def dot(left, right, dims=NN):
    return lax.dot_general(left, right, dims, preferred_element_type=F32)


def from_other(part):
    half = part.shape[0] // 2
    other = swapped(part.astype(BF)).astype(F32)
    return jnp.concatenate([other[half:], other[:half]])


class Forward:
    def __init__(self, start, ring, marks, norms, received=None):
        self.ring, self.marks, self.norms = ring, marks, norms
        self.start, self.received = start, received
        self.rows = start.shape[0]

    def norm(self, earlier=None):
        hidden_low = self.start
        if self.received is not None:
            received = after(self.received, earlier)
            hidden_low = jnp.where(lax.axis_index("section") == 0, self.start, received)
        self.hidden = hidden_low.astype(F32)
        self.hidden_other = swapped(hidden_low)
        normed = layer_norm(self.hidden, self.norms[0], self.norms[1]).astype(BF)
        self.normed = normed
        self.near = fetched(normed, self.ring, 1), fetched(normed, self.ring, 3)

    def fetch_raw(self, earlier):
        self.hidden_low = after(self.start, earlier)
        self.hidden_other = swapped(self.hidden_low)
        self.near = fetched(self.hidden_low, self.ring, 1), fetched(self.hidden_low, self.ring, 3)
        self.fetch_far()

    def collect_raw(self):
        self.hidden = self.hidden_low.astype(F32)
        plus, minus = self.near
        ring_rows = jnp.concatenate([self.hidden_low, plus, *self.far, minus])
        rows = jnp.concatenate([ring_rows, swapped(ring_rows)]).astype(F32)
        self.normed_all = layer_norm(rows, self.norms[0], self.norms[1]).astype(BF)
        half = 4 * self.rows
        self.normed_chip = jnp.concatenate(
            [self.normed_all[: self.rows], self.normed_all[half : half + self.rows]]
        )

    def swap_near(self):
        plus, minus = self.near
        self.other_near = swapped(jnp.concatenate([self.normed, plus, minus]))

    def fetch_far(self):
        plus, minus = self.near
        half = self.rows // 2
        self.far = fetched(plus[:half], self.ring, 1), fetched(minus[half:], self.ring, 3)

    def collect(self, earlier=None):
        rows, normed = self.rows, self.normed
        plus, minus = self.near
        two = jnp.concatenate(after(self.far, earlier))
        other_near, other_two = self.other_near, swapped(two)
        self.normed_all = jnp.concatenate(
            [normed, plus, two, minus, other_near[: 2 * rows], other_two, other_near[2 * rows :]]
        )
        self.normed_chip = jnp.concatenate([normed, other_near[:rows]])

    def project(self, weights, earlier):
        normed_all, normed_chip = after((self.normed_all, self.normed_chip), earlier)
        self.kv = dot(normed_all, weights["kv"]).astype(BF)
        self.q = dot(normed_chip, weights["q"]).astype(BF)

    def attention(self, save):
        self.attended, *self.lse = attend(self.q, self.kv, *self.marks, save)

    def feed_forward(self, weights, save, arrivals, between):
        rows = self.rows
        part = dot(self.attended, weights["out"])
        hidden = jnp.concatenate([self.hidden, self.hidden_other.astype(F32)])
        self.middle = hidden + part + from_other(part)
        normed_ffn = layer_norm(self.middle, self.norms[2], self.norms[3]).astype(BF)
        self.normed_ffn = after(normed_ffn, arrivals)
        fed, self.act, *self.slope = feed(self.normed_ffn, weights["feed"], save)
        self.fed = fed = after(fed, between)
        self.result = (self.middle[:rows] + fed[:rows] + swapped(fed[rows:].astype(BF)).astype(F32)).astype(BF)


class Backward:
    def __init__(self, grad_low, forward):
        self.grad_low, self.forward = grad_low, forward
        self.rows = grad_low.shape[0]
        self.grad_chip = jnp.concatenate([grad_low, swapped(grad_low)])

    def feed_forward(self, weights, earlier, arrivals):
        rows, forward = self.rows, self.forward
        grad_chip = after(self.grad_chip, earlier)
        back, self.grad_up = feed_back(grad_chip, *forward.slope, weights["feed"])
        back = after(back, arrivals)
        grad_normed = back + from_other(back)
        gain = forward.norms[2]
        part, unit = layer_norm_back(forward.middle, gain, grad_normed)
        self.grad_gain_ffn = jnp.sum(grad_normed[:rows] * unit[:rows], axis=0)
        self.grad_bias_ffn = jnp.sum(grad_normed[:rows], axis=0)
        grad_middle = grad_chip.astype(F32) + part
        self.grad_middle = grad_middle[:rows]
        self.grad_middle_low = grad_middle.astype(BF)
        self.grad_heads = dot(self.grad_middle_low, weights["out"], NT).astype(BF)

    def attention(self, earlier):
        forward = self.forward
        grad_heads = after(self.grad_heads, earlier)
        self.dq, self.dkv = attend_back(
            forward.q, forward.kv, grad_heads, forward.attended, *forward.lse, *forward.marks
        )

    def project(self, weights, earlier=None):
        dq, dkv = after((self.dq, self.dkv), earlier)
        self.own, self.away = project_back(dq, dkv, weights["q"], weights["kv"])

    def sum_cores(self, earlier=None):
        rows = self.rows
        own, away = after((self.own, self.away), earlier)
        far = swapped(away[2 * rows : 3 * rows])
        near = swapped(jnp.concatenate([away[: 2 * rows], away[3 * rows :]]))
        self.ring_grads = [
            own[d * rows : (d + 1) * rows] + part.astype(F32)
            for d, part in enumerate((near[:rows], near[rows : 2 * rows], far, near[2 * rows :]))
        ]

    def piece(self, steps, lower=0, upper=None):
        return self.ring_grads[steps][lower : self.rows if upper is None else upper]

    def spread_far(self):
        half, ring = self.rows // 2, self.forward.ring
        self.far = (
            moved(self.piece(2, 0, half).astype(BF), ring, 1),
            moved(self.piece(2, half).astype(BF), ring, -1),
        )

    def spread_near(self, earlier=None):
        half, ring = self.rows // 2, self.forward.ring
        from_left, from_right = after(self.far, earlier)
        right = jnp.concatenate([self.piece(1, 0, half) + from_left.astype(F32), self.piece(1, half)])
        left = jnp.concatenate([self.piece(3, 0, half), self.piece(3, half) + from_right.astype(F32)])
        self.near = moved(right.astype(BF), ring, 1), moved(left.astype(BF), ring, -1)

    def reduce(self, earlier=None):
        forward = self.forward
        grad_normed = self.piece(0)
        for part in after(self.near, earlier):
            grad_normed = grad_normed + part.astype(F32)
        part, unit = layer_norm_back(forward.hidden, forward.norms[0], grad_normed)
        self.grad_gain_attn = jnp.sum(grad_normed * unit, axis=0)
        self.grad_bias_attn = jnp.sum(grad_normed, axis=0)
        self.grad_hidden_low = (self.grad_middle + part).astype(BF)

    def vectors(self):
        return jnp.stack([self.grad_gain_attn, self.grad_bias_attn, self.grad_gain_ffn, self.grad_bias_ffn])


def marks_of(lengths, place, rows, core):
    index = lax.iota(jnp.int32, 8 * rows)
    core_at = jnp.where(index < 4 * rows, core, 1 - core)
    chip_at = lax.rem(place + lax.rem(index // rows, 4), 4)
    positions = chip_at * (2 * rows) + core_at * rows + lax.rem(index, rows)
    cells = lengths.shape[0]
    bounds = jnp.cumsum(lengths)
    segments = jnp.sum((positions[:, None] >= bounds[None, :]).astype(jnp.int32), axis=1, keepdims=True)
    places = lax.broadcasted_iota(jnp.int32, (1, 128), 1)
    own = segments == places
    mark_q = jnp.where(own | (places >= cells), 0.0, MASKED).astype(BF)
    mark_k = own.astype(BF)
    return jnp.concatenate([mark_q[:rows], mark_q[4 * rows : 5 * rows]]), mark_k


def arrange_kernel(qkv_ref, out_ref, vectors_ref, mine_ref, other_ref):
    width = out_ref.shape[1]
    half = width // 2
    core = lax.axis_index("core")
    for at_core, target in ((core, mine_ref), (1 - core, other_ref)):
        start = at_core * half

        def columns(base, size):
            return pl.ds(pl.multiple_of(start + base, 128), size)

        for pair in range(half // 128):
            target[:, 256 * pair : 256 * pair + 128] = qkv_ref[:, columns(width + 128 * pair, 128)]
            target[:, 256 * pair + 128 : 256 * pair + 256] = qkv_ref[:, columns(2 * width + 128 * pair, 128)]
        target[:, width : width + half] = qkv_ref[:, columns(0, half)]
        target[:, width + half : 2 * width] = out_ref[:, columns(0, half)]
        target[:, 2 * width :] = vectors_ref[...]


def attention_shards(w_qkv, w_out, vectors, core_zero):
    rows, width = w_out.shape
    columns = jnp.pad(vectors.T, ((0, 0), (0, 128 - vectors.shape[0])))
    out_shape = [jax.ShapeDtypeStruct((rows, 2 * width + 128), BF)] * 2
    mine, other = called(arrange_kernel, "arrange", out_shape, (w_qkv, w_out, columns), 0, 0)
    other = swapped(other)
    both = jnp.concatenate([picked(core_zero, mine, other), picked(core_zero, other, mine)])
    return both[:, :width], both[:, width:]


def exchanged_in(zero, one, core_zero):
    mine = picked(core_zero, zero, one)
    other = swapped(picked(core_zero, one, zero))
    return jnp.concatenate([picked(core_zero, mine, other), picked(core_zero, other, mine)])


def feed_shard(w_up, w_down, core_zero):
    rows = w_up.shape[0]
    units = w_up.reshape(rows, 16, 2, 2, -1).transpose(2, 0, 3, 1, 4).reshape(2, rows, -1)
    up = exchanged_in(units[0], units[1], core_zero)
    half = w_down.shape[0] // 2
    return jnp.concatenate([up, w_down[:half], w_down[half:]], axis=1)


def out_rows(out_half, core_zero):
    half = out_half.shape[1]
    zero, one = out_half[:half], out_half[half:]
    mine = picked(core_zero, zero, one)
    other = swapped(picked(core_zero, one, zero))
    return jnp.concatenate([picked(core_zero, mine, other), picked(core_zero, other, mine)], axis=1)


TN = (((0,), (0,)), ((), ()))


def summed(lefts, rights):
    return dot(jnp.concatenate(lefts), jnp.concatenate(rights), TN)


def feed_grads(backs):
    forwards = [back.forward for back in backs]
    width = backs[0].grad_chip.shape[1]
    up = summed([f.normed_ffn for f in forwards], [back.grad_up for back in backs])
    act = jnp.concatenate([f.act for f in forwards])
    grads = jnp.concatenate([back.grad_chip for back in backs])
    down = [dot(act[:, h * width : (h + 1) * width], grads, TN) for h in range(2)]
    return jnp.concatenate([up.astype(BF)] + [part.astype(BF) for part in down], axis=1)


def out_grads(backs, core_zero):
    grads = summed([back.forward.attended for back in backs], [back.grad_middle_low for back in backs])
    grads = grads.astype(BF)
    half = grads.shape[0]
    zero, one = grads[:, :half], grads[:, half:]
    mine = picked(core_zero, zero, one)
    other = swapped(picked(core_zero, one, zero))
    return jnp.concatenate([picked(core_zero, mine, other), picked(core_zero, other, mine)])


def query_grads(backs):
    return summed([back.forward.normed_chip for back in backs], [back.dq for back in backs]).astype(BF)


def key_value_grads(backs, earlier):
    dkv = after([back.dkv for back in backs], earlier)
    return summed([back.forward.normed_all for back in backs], dkv).astype(BF)


def vector_grads(backs):
    vectors = sum(back.vectors() for back in backs)
    vectors = jnp.pad(vectors, ((0, 128 - vectors.shape[0]), (0, 0))).astype(BF)
    return added(vectors, swapped(vectors)).T


def exchanged_out(shard, core_zero):
    rows = shard.shape[0] // 2
    zero, one = shard[:rows], shard[rows:]
    mine = picked(core_zero, zero, one)
    other = swapped(picked(core_zero, one, zero).astype(BF)).astype(F32)
    return picked(core_zero, mine, other), picked(core_zero, other, mine)


SOURCES = ((1, 2), (2, 1), (3, 0))


def whole_features(inputs, cotangents, section):
    turned = transposed(jnp.stack([inputs[1], cotangents[1]]))
    inputs = jnp.stack([inputs[0], turned[0]])
    cotangents = jnp.stack([cotangents[0], turned[1]])
    one, two, three = (
        lax.ppermute(picked(section == a, inputs, cotangents), "section", [(a, 0), (b, 3)]) for a, b in SOURCES
    )
    start = jnp.concatenate([inputs, one, two, three], axis=2)
    last = jnp.concatenate([three, two, one, cotangents], axis=2)
    return start, last


def spread_features(grads, outputs, section):
    width = grads.shape[2] // 4

    def piece(value, z):
        return value[:, :, z * width : (z + 1) * width]

    one, two, three = (
        lax.ppermute(picked(section == 0, piece(grads, a), piece(outputs, b)), "section", [(0, a), (3, b)])
        for a, b in SOURCES
    )

    def by_section(values):
        result = values[3]
        for z in range(3):
            result = jnp.where(section == z, values[z], result)
        return result

    grads = by_section((piece(grads, 0), one, two, three))
    outputs = by_section((three, two, one, piece(outputs, 3)))
    turned = transposed(jnp.stack([grads[1], outputs[1]]))
    return jnp.stack([grads[0], turned[0]]), jnp.stack([outputs[0], turned[1]])


def local(
    block_input,
    cotangent,
    cell_lengths,
    norm_attn_gain,
    norm_attn_bias,
    w_qkv,
    w_out,
    norm_ffn_gain,
    norm_ffn_bias,
    w_up,
    w_down,
):
    section = lax.axis_index("section")
    at_x = lax.axis_index("dp")
    at_y = lax.axis_index("y")
    core = lax.axis_index("core")
    core_zero = core == 0
    sections = lax.axis_size("section")
    rows = block_input.shape[1]
    rings = ("y", "dp")
    width = w_out.shape[2]
    half = width // 2

    feed_whole = lax.all_gather(feed_shard(w_up[0], w_down[0], core_zero), ("dp", "y"), axis=0, tiled=True)
    vectors = jnp.concatenate([norm_attn_gain, norm_attn_bias, norm_ffn_gain, norm_ffn_bias])
    kv_shard, rest_shard = attention_shards(w_qkv[0], w_out[0], vectors, core_zero)
    kv, rest = Gather([kv_shard], "dp", "y"), Gather([rest_shard], "y", "dp")
    start, last_grad = whole_features(block_input, cotangent, section)
    passes = [Forward(start[m], rings[m], None, None) for m in range(2)]
    kv.neighbours((start, last_grad))
    rest.neighbours((start, last_grad))
    kv.along_first()
    rest.along_first()
    near = kv.along_second() + rest.along_second()
    for now in passes:
        now.fetch_raw(near)
    marks = (
        marks_of(cell_lengths[2 * at_x], at_y, rows, core),
        marks_of(cell_lengths[2 * at_y + 1], at_x, rows, core),
    )
    (w_kv,) = kv.placed()
    (rest_whole,) = rest.placed()
    weights = {"kv": w_kv, "q": rest_whole[:, :half], "out": out_rows(rest_whole[:, half:width], core_zero)}
    norms = rest_whole[:, width:].T[:4].astype(F32)
    norms = tuple(norms[i : i + 1] for i in range(4))
    for m, now in enumerate(passes):
        now.marks, now.norms = marks[m], norms
        now.collect_raw()
    weights["feed"] = feed_whole

    forward_pairs = [(s, s + 1) for s in range(sections - 1)]
    result = None
    for step in range(sections):
        final = step == sections - 1
        for m in range(2):
            now, other = passes[m], passes[1 - m]
            waiting = step + m > 0 and not (final and m == 1)
            now.project(weights, result)
            now.attention(final)
            if waiting:
                other.norm(now.attended)
                now.attended = after(now.attended, other.normed)
                other.swap_near()
                other.fetch_far()
            now.feed_forward(
                weights, final, other.near if waiting else None, other.other_near if waiting else None
            )
            if waiting:
                other.collect(now.fed)
            result = now.result
            if not final:
                received = lax.ppermute(result, "section", forward_pairs)
                passes[m] = Forward(start[m], rings[m], marks[m], norms, received)
    block_output = jnp.stack([now.result for now in passes])

    backs = [Backward(last_grad[m], passes[m]) for m in range(2)]
    backward_pairs = [(s + 1, s) for s in range(sections - 1)]
    earlier = result
    for step in range(sections):
        final = step == sections - 1
        for m in range(2):
            now, other = backs[m], backs[1 - m]
            waiting = step + m > 0
            now.feed_forward(weights, earlier, other.far if waiting else None)
            if waiting:
                other.spread_near()
            if final and m == 1:
                break
            now.attention(None)
            if waiting:
                other.reduce(now.dkv)
                now.project(weights, other.grad_hidden_low)
                received = lax.ppermute(other.grad_hidden_low, "section", backward_pairs)
                received = after(received, now.own)
                grad_low = jnp.where(section == sections - 1, last_grad[1 - m], received)
                backs[1 - m] = Backward(grad_low, passes[1 - m])
                now.sum_cores(grad_low)
            else:
                now.project(weights)
                now.sum_cores()
            now.spread_far()
            earlier = now.ring_grads

    joint = feed_grads(backs)
    backs[0].reduce(backs[1].grad_up)
    backs[1].attention((backs[0].grad_hidden_low, joint))
    joint = lax.psum_scatter(joint, ("dp", "y"), scatter_dimension=0, tiled=True).astype(F32)
    backs[1].project(weights)
    backs[1].sum_cores()
    backs[1].spread_far()
    backs[1].spread_near()
    kv_part = key_value_grads(backs, backs[1].far)
    out_part = out_grads(backs, core_zero)
    query_part = query_grads(backs)
    backs[1].reduce((kv_part, query_part))
    sum_kv = Scatter([after(kv_part, backs[1].near)], "y", "dp")
    sum_rest = Scatter([query_part, out_part, vector_grads(backs)], "dp", "y")
    sum_kv.far()
    sum_rest.far()
    sum_kv.near()
    sum_rest.near()
    mine = sum_kv.bundle(), sum_rest.bundle()
    sum_kv.mine, sum_rest.mine = after(mine, mine[::-1])
    small = sum_kv.small_far() + sum_rest.small_far()
    own_rows = w_out.shape[1]
    up_grads = joint[:, : 2 * width]
    grad_down = jnp.concatenate([joint[:, 2 * width : 3 * width], joint[:, 3 * width :]])
    units = jnp.stack(exchanged_out(up_grads, core_zero), axis=1)
    units = units.reshape(own_rows, 2, 2, 16, -1).transpose(0, 3, 1, 2, 4)
    grad_up = units.reshape(own_rows, -1)
    input_grad = after(jnp.stack([now.grad_hidden_low for now in backs]), small)
    input_grad, block_output = spread_features(input_grad, block_output, section)
    kv_grads = after(sum_kv.total(), grad_up)
    rest_grads = sum_rest.total()

    kv_cores = exchanged_out(kv_grads, core_zero)
    rest_cores = exchanged_out(rest_grads[:, :width], core_zero)
    keys, values = [], []
    for part in kv_cores:
        for pair in range(half // 128):
            keys.append(part[:, 256 * pair : 256 * pair + 128])
            values.append(part[:, 256 * pair + 128 : 256 * pair + 256])
    grad_qkv = jnp.concatenate([rest_cores[0][:, :half], rest_cores[1][:, :half]] + keys + values, axis=1)
    grad_out = jnp.concatenate([rest_cores[0][:, half:width], rest_cores[1][:, half:width]], axis=1)
    columns = rest_grads[:, width:]
    grad_vectors = picked(core_zero, columns[:own_rows], columns[own_rows:]).T[:4]
    return (
        block_output,
        input_grad.astype(F32),
        grad_vectors[0:1],
        grad_vectors[1:2],
        grad_qkv[None],
        grad_out[None],
        grad_vectors[2:3],
        grad_vectors[3:4],
        grad_up[None],
        grad_down[None],
    )


def solution(mesh):
    sizes = mesh.devices.shape
    cores = Mesh(mesh.devices.reshape(sizes[0], sizes[1], sizes[2] // 2, 2), ("section", "dp", "y", "core"))
    seq = ("y", "core")
    plane = ("dp", "y", "core")
    rows = P("dp", seq, "section")
    vector = P("section", plane)
    matrix = P("section", plane, None)
    return jax.shard_map(
        local,
        mesh=cores,
        in_specs=(rows, rows, P(), vector, vector, matrix, matrix, vector, vector, matrix, matrix),
        out_specs=(rows, rows, vector, vector, matrix, matrix, vector, vector, matrix, matrix),
        check_vma=False,
    )
```
